32 devices in a mesh: tm: 16 (over z, y, x), span: 2 (over core).
Axes of the slice: x: 2, y: 2, z: 4, core: 2. Of those that a mesh axis runs over, the one named last changes fastest.
Arguments:
- frames: bfloat16 [16, 64, 64, 128], P('tm', None, 'span'), may hold values from -6 to 6
- cotangent: bfloat16 [16, 64, 64, 128], P('tm', None, 'span'), may hold values from -6 to 6
- spatial_weight: bfloat16 [3, 3, 64, 64], replicated, may hold values from -0.25 to 0.25
- temporal_kernel: bfloat16 [64, 16], replicated, may hold values from -1.5 to 1.5
Outputs:
- block_output: bfloat16 [16, 64, 64, 128], P('tm', None, 'span')
- input_grad: bfloat16 [16, 64, 64, 128], P('tm', None, 'span')
- weight_grad: float32 [3, 3, 64, 64], replicated
- kernel_grad: float32 [64, 16], replicated
The draws below stay inside these ranges and needn't reach their ends.
All inputs are finite; a program needn't handle non-finite values.
Results may differ from the reference program's by a relative error of at most 0.0051.
Values may be sent and summed in bfloat16 or wider, within the bound.
No kernel may reach another device: no remote copies, remote signals or barrier semaphores. Data moves between devices by JAX's collectives and lax.ppermute only.
A program may use at most 64 MiB of HBM per device.

```python
import jax
import jax.numpy as jnp
from jax import lax

C = 64
CW = 128
TF = 16
SP = 64


def block_scale(key, dims, pieces, smallest, largest):
    def one(position, shards_of):
        heights = jax.random.uniform(jax.random.fold_in(jax.random.fold_in(key, 6), position), (shards_of,), jnp.float32, smallest / len(pieces), largest / len(pieces))
        return jnp.repeat(jnp.exp(heights), dims[position] // shards_of).reshape((-1,) + (1,) * (len(dims) - position - 1))

    level = one(*pieces[0])
    for cut in pieces[1:]:
        level = level * one(*cut)
    return level


def centred(stream_key, extent, spread, limit, pieces=(), kind=jnp.bfloat16):
    entries = jax.random.normal(stream_key, extent, jnp.float32) * spread
    if len(pieces) > 0:
        entries = block_scale(stream_key, extent, pieces, -0.22, 0.18) * entries
    return jnp.clip(entries, min=-limit, max=limit).astype(kind)


def setup_inputs(seed: int = 0) -> dict:
    arg_keys = jax.random.split(jax.random.key(seed), 5)
    frames = centred(arg_keys[0], (TF, C, SP, CW), 1.0, 6.0, ((0, 16), (2, 2)))
    cotangent = centred(arg_keys[1], (TF, C, SP, CW), 1.0, 6.0, ((0, 16), (2, 2)))
    spatial_weight = centred(arg_keys[2], (3, 3, C, C), (9 * C) ** -0.5, 0.25)
    temporal_kernel = centred(arg_keys[3], (C, TF), TF ** -0.5, 1.5)
    return dict(frames=frames, cotangent=cotangent, spatial_weight=spatial_weight, temporal_kernel=temporal_kernel)


def toeplitz(kernel):
    count = kernel.shape[1]
    chans = kernel.shape[0]
    vector = jnp.concatenate([jnp.zeros((chans, 1), kernel.dtype), kernel[:, ::-1], jnp.zeros((chans, count - 1), kernel.dtype)], axis=1)
    tiled = jnp.tile(vector, (1, count))
    skewed = tiled[:, count:count + count * (2 * count - 1)].reshape(chans, count, 2 * count - 1)
    return skewed[:, :, :count]


def diagonal_sums(products):
    chans = products.shape[0]
    count = products.shape[1]
    flipped = products[:, :, ::-1]
    wide = jnp.concatenate([flipped, jnp.zeros_like(flipped)], axis=2)
    skewed = wide.reshape(chans, 2 * count * count)[:, :count * (2 * count - 1)].reshape(chans, count, 2 * count - 1)
    return jnp.sum(skewed[:, :, count - 1:], axis=1)


def convolve(field, weights):
    return lax.conv_general_dilated(field[None], weights, (1, 1), ((1, 1), (1, 1)), dimension_numbers=("NCHW", "OIHW", "NCHW"))[0]


def reference(frames, cotangent, spatial_weight, temporal_kernel):
    forward_w = spatial_weight.astype(jnp.float32).transpose(2, 3, 0, 1)
    flipped_w = spatial_weight.astype(jnp.float32)[::-1, ::-1].transpose(3, 2, 0, 1)
    gscale = float(TF * SP * CW) ** -0.5

    def activate(frame):
        hidden = convolve(frame.astype(jnp.float32), forward_w)
        return (hidden * jax.nn.sigmoid(hidden)).astype(jnp.bfloat16)

    active = lax.map(activate, frames)
    toe = toeplitz(temporal_kernel).astype(jnp.float32)
    flat_act = active.reshape(TF, C, SP * CW).astype(jnp.float32)
    flat_cot = cotangent.reshape(TF, C, SP * CW).astype(jnp.float32)
    along = jnp.einsum("cts,scn->tcn", toe, flat_act).astype(jnp.bfloat16)
    block_output = (frames.astype(jnp.float32) + along.reshape(frames.shape).astype(jnp.float32)).astype(jnp.bfloat16)
    back = jnp.einsum("cts,tcn->scn", toe, flat_cot).astype(jnp.bfloat16).reshape(frames.shape)
    kernel_grad = diagonal_sums(jnp.einsum("tcn,scn->cts", flat_cot, flat_act)) * gscale

    def backward(carry, inputs):
        frame, cot_frame, back_frame = inputs
        field = frame.astype(jnp.float32)
        hidden = convolve(field, forward_w)
        sigma = jax.nn.sigmoid(hidden)
        dhidden = (back_frame.astype(jnp.float32) * sigma * (1.0 + hidden * (1.0 - sigma))).astype(jnp.bfloat16)
        dfield = dhidden.astype(jnp.float32)
        grad_frame = (cot_frame.astype(jnp.float32) + convolve(dfield, flipped_w)).astype(jnp.bfloat16)
        padded = jnp.pad(field, ((0, 0), (1, 1), (1, 1)))
        terms = jnp.stack([jnp.einsum("osw,isw->oi", dfield, padded[:, row_off:row_off + SP, col_off:col_off + CW]) for row_off in range(3) for col_off in range(3)]).reshape(3, 3, C, C)
        return carry + terms, grad_frame

    weight_sum, input_grad = lax.scan(backward, jnp.zeros((3, 3, C, C), jnp.float32), (frames, cotangent, back))
    return block_output, input_grad, weight_sum * gscale, kernel_grad
```

```python
import functools

import jax
import jax.numpy as jnp
from jax import lax
from jax.experimental import pallas as pl
from jax.experimental.pallas import tpu as pltpu
from jax.sharding import PartitionSpec as P

F32 = jnp.float32
BF16 = jnp.bfloat16
VMEM_LIMIT = 40 * 1024 * 1024


def call(body, out, scratch, flops, nbytes):
    return pl.pallas_call(
        body,
        out_shape=out,
        scratch_shapes=scratch,
        compiler_params=pltpu.CompilerParams(vmem_limit_bytes=VMEM_LIMIT),
        cost_estimate=pl.CostEstimate(flops=flops, bytes_accessed=nbytes, transcendentals=0),
    )


def shifted(x, back):
    width = x.shape[-1]
    lane = lax.broadcasted_iota(jnp.int32, x.shape, x.ndim - 1)
    wide = x.astype(F32)
    if back:
        moved = jnp.where(lane == 0, 0.0, pltpu.roll(wide, 1, x.ndim - 1))
    else:
        moved = jnp.where(lane == width - 1, 0.0, pltpu.roll(wide, width - 1, x.ndim - 1))
    return moved.astype(x.dtype)


def fill_padded(pad_ref, before_ref, x_ref, after_ref):
    rows = x_ref.shape[0]
    pad_ref[0] = before_ref[...]
    pad_ref[pl.ds(1, rows)] = x_ref[...]
    pad_ref[rows + 1] = after_ref[...]


def conv_partials(pad_ref, weight_ref, part_ref, flip):
    weight = weight_ref[...]

    def two(step, carry):
        rows = []
        for k in range(2):
            x = pad_ref[2 * step + k]
            rows.append(jnp.concatenate([shifted(x, not flip), x, shifted(x, flip)], axis=0))
        both = jnp.concatenate(rows, axis=1)
        got = jnp.dot(weight, both, preferred_element_type=F32)
        width = got.shape[1] // 2
        part_ref[2 * step] = got[:, :width]
        part_ref[2 * step + 1] = got[:, width:]
        return carry

    lax.fori_loop(0, pad_ref.shape[0] // 2, two, 0, unroll=True)


def forward_body(before_ref, x_ref, after_ref, weight_ref, active_ref, slope_ref, pad_ref, part_ref):
    rows, channels, width = x_ref.shape
    fill_padded(pad_ref, before_ref, x_ref, after_ref)
    conv_partials(pad_ref, weight_ref, part_ref, False)

    def one(row, carry):
        hidden = (
            part_ref[row, :channels]
            + part_ref[row + 1, channels : 2 * channels]
            + part_ref[row + 2, 2 * channels :]
        )
        sigma = 1.0 / (1.0 + jnp.exp(-hidden))
        active_ref[row] = (hidden * sigma).astype(BF16)
        slope_ref[row] = sigma * (1.0 + hidden * (1.0 - sigma))
        return carry

    lax.fori_loop(0, rows, one, 0, unroll=4)


def input_grad_body(before_ref, d_ref, after_ref, weight_ref, cot_ref, out_ref, pad_ref, part_ref):
    rows, channels, width = d_ref.shape
    fill_padded(pad_ref, before_ref, d_ref, after_ref)
    conv_partials(pad_ref, weight_ref, part_ref, True)

    def one(row, carry):
        total = (
            part_ref[row + 2, :channels]
            + part_ref[row + 1, channels : 2 * channels]
            + part_ref[row, 2 * channels :]
        )
        out_ref[row] = (cot_ref[row].astype(F32) + total).astype(BF16)
        return carry

    lax.fori_loop(0, rows, one, 0, unroll=4)


def chunk_place(index, channels):
    per_row = channels // 16
    start = pl.multiple_of((index % per_row) * 16, 16)
    return index // per_row, pl.ds(start, 16)


def back_body(cot_ref, coef_ref, back_ref):
    frames, tile_rows, channels, width = cot_ref.shape

    def one(index, carry):
        row, chans = chunk_place(index, channels)
        cot = [cot_ref[t, row, chans].astype(F32) for t in range(frames)]
        coef = [coef_ref[l, chans] for l in range(frames)]
        for r in range(frames):
            total = coef[0] * cot[r]
            for t in range(r + 1, frames):
                total = total + coef[t - r] * cot[t]
            back_ref[r, row, chans] = total.astype(BF16)
        return carry

    lax.fori_loop(0, tile_rows * (channels // 16), one, 0)


def along_body(act_ref, cot_ref, coef_ref, along_ref, grad_ref, sum_ref):
    frames, tile_rows, channels, width = cot_ref.shape
    sum_ref[...] = jnp.zeros_like(sum_ref)

    def one(index, carry):
        row, chans = chunk_place(index, channels)
        act = [act_ref[t, row, chans].astype(F32) for t in range(frames)]
        coef = [coef_ref[l, chans] for l in range(frames)]
        for t in range(frames):
            total = coef[0] * act[t]
            for r in range(t):
                total = total + coef[t - r] * act[r]
            along_ref[t, row, chans] = total.astype(BF16)
        cot = [cot_ref[t, row, chans].astype(F32) for t in range(frames)]
        for lag in range(frames):
            total = cot[lag] * act[0]
            for t in range(lag + 1, frames):
                total = total + cot[t] * act[t - lag]
            sum_ref[lag, chans] += total
        return carry

    lax.fori_loop(0, tile_rows * (channels // 16), one, 0)
    grad_ref[...] = jnp.sum(sum_ref[...], axis=2)


def weight_grad_body(
    back_ref, slope_ref, before_ref, x_ref, after_ref, dhid_ref, grad_ref, pad_ref, dpad_ref
):
    rows, channels, width = x_ref.shape
    fill_padded(pad_ref, before_ref, x_ref, after_ref)
    zero = jnp.zeros((2, channels, width), BF16)
    dpad_ref[pl.ds(0, 2)] = zero
    dpad_ref[pl.ds(rows + 2, 2)] = zero

    def one(row, carry):
        value = (back_ref[row].astype(F32) * slope_ref[row]).astype(BF16)
        dhid_ref[row] = value
        dpad_ref[row + 2] = value
        return carry

    lax.fori_loop(0, rows, one, 0, unroll=4)
    grad_ref[...] = jnp.zeros_like(grad_ref)

    def two(step, carry):
        left, right = [], []
        for k in range(2):
            row = 2 * step + k
            x = pad_ref[row]
            right.append(jnp.concatenate([shifted(x, True), x, shifted(x, False)], axis=0))
            left.append(jnp.concatenate([dpad_ref[row + 2], dpad_ref[row + 1], dpad_ref[row]], axis=0))
        grad_ref[...] += lax.dot_general(
            jnp.concatenate(left, axis=1),
            jnp.concatenate(right, axis=1),
            (((1,), (1,)), ((), ())),
            preferred_element_type=F32,
        )
        return carry

    lax.fori_loop(0, (rows + 2) // 2, two, 0, unroll=True)


def edges(x):
    size = lax.axis_size("span")
    up = [(i, (i + 1) % size) for i in range(size - 1)]
    down = [(j, i) for i, j in up]
    return lax.ppermute(x[-1], "span", up), lax.ppermute(x[0], "span", down)


def tree_sum(parts):
    while len(parts) > 1:
        parts = [parts[i] + parts[i + 1] for i in range(0, len(parts), 2)]
    return parts[0]


def xor_sum(x, axis, steps):
    size = lax.axis_size(axis)
    return tree_sum([x] + [lax.ppermute(x, axis, [(i, i ^ k) for i in range(size)]) for k in steps[1:]])


def total_over_all(x):
    size = lax.axis_size("span")
    count = lax.axis_size("tm")
    rows = x.shape[0]
    half = -(-rows // 16) * 8
    x = jnp.pad(x, ((0, 2 * half - rows), (0, 0)))
    low = lax.axis_index("span") % 2 == 0
    swap = [(i, i ^ 1) for i in range(size)]
    mine = jnp.where(low, x[:half], x[half:])
    other = jnp.where(low, x[half:], x[:half])
    mine = mine + lax.ppermute(other, "span", swap)
    if size > 2:
        mine = xor_sum(mine, "span", list(range(0, size, 2)))
    plane = min(4, count)
    mine = xor_sum(mine, "tm", list(range(plane)))
    if count > plane:
        mine = xor_sum(mine, "tm", list(range(0, count, plane)))
    other = lax.ppermute(mine, "span", swap)
    first = jnp.where(low, mine, other)
    second = jnp.where(low, other, mine)
    return jnp.concatenate([first, second], axis=0)[:rows]


def local(frames, cotangent, spatial_weight, temporal_kernel):
    channels, rows, width = frames.shape[1:]
    count = lax.axis_size("tm")
    gscale = float(count * rows * lax.axis_size("span") * width) ** (-0.5)
    share = rows // count
    shape = (rows, channels, width)
    tile = (count, share, channels, width)
    area = rows * width
    act_bytes = channels * area * 2

    def exchange(x):
        return lax.all_to_all(x.reshape(tile), "tm", split_axis=0, concat_axis=0, tiled=True)

    cot = cotangent[0].transpose(1, 0, 2)
    cot_tile = exchange(cot)
    x = frames[0].transpose(1, 0, 2)
    x_before, x_after = edges(x)
    weight = spatial_weight.transpose(0, 2, 1, 3).reshape(3 * channels, 3 * channels)
    weight_back = spatial_weight.transpose(0, 3, 1, 2).reshape(3 * channels, 3 * channels)
    coef = jnp.broadcast_to(temporal_kernel.T.astype(F32)[:, :, None], (count, channels, width))
    pad = pltpu.VMEM((rows + 2, channels, width), BF16)
    part = pltpu.VMEM((rows + 2, 3 * channels, width), F32)
    flops = 18 * channels * channels * area
    active, slope = call(
        forward_body,
        (jax.ShapeDtypeStruct(shape, BF16), jax.ShapeDtypeStruct(shape, F32)),
        [pad, part],
        flops,
        4 * act_bytes,
    )(x_before, x, x_after, weight)
    back = call(back_body, jax.ShapeDtypeStruct(tile, BF16), [], 17 * channels * area, 2 * act_bytes)(
        cot_tile, coef
    )
    back = exchange(back).reshape(shape)
    act_tile = exchange(active)
    along, kernel_local = call(
        along_body,
        (jax.ShapeDtypeStruct(tile, BF16), jax.ShapeDtypeStruct((count, channels), F32)),
        [pltpu.VMEM((count, channels, width), F32)],
        34 * channels * area,
        3 * act_bytes,
    )(act_tile, cot_tile, coef)
    along = exchange(along).reshape(shape)
    dhidden, weight_local = call(
        weight_grad_body,
        (
            jax.ShapeDtypeStruct(shape, BF16),
            jax.ShapeDtypeStruct((3 * channels, 3 * channels), F32),
        ),
        [pad, pltpu.VMEM((rows + 4, channels, width), BF16)],
        flops,
        5 * act_bytes,
    )(back, slope, x_before, x, x_after)
    d_before, d_after = edges(dhidden)
    input_grad = call(
        input_grad_body, jax.ShapeDtypeStruct(shape, BF16), [pad, part], flops, 4 * act_bytes
    )(d_before, dhidden, d_after, weight_back, cot)
    block_output = (x.astype(F32) + along.astype(F32)).astype(BF16)
    sums = jnp.concatenate([weight_local.reshape(-1), kernel_local.reshape(-1)])
    total = total_over_all(sums.reshape(-1, 128)).reshape(-1) * gscale
    weights = 9 * channels * channels
    weight_total = total[:weights].reshape(3, channels, 3, channels).transpose(0, 2, 1, 3)
    kernel_total = total[weights:].reshape(count, channels).T
    return (
        block_output.transpose(1, 0, 2)[None],
        input_grad.transpose(1, 0, 2)[None],
        weight_total,
        kernel_total,
    )


def solution(mesh):
    placed = (P("tm", None, "span", None), P("tm", None, "span", None), P(), P())
    return jax.shard_map(
        local,
        mesh=mesh,
        in_specs=placed,
        out_specs=(P("tm", None, "span", None), P("tm", None, "span", None), P(), P()),
        check_vma=False,
    )
```

```python
import functools

import jax
import jax.numpy as jnp
from jax import lax
from jax.experimental import pallas as pl
from jax.experimental.pallas import tpu as pltpu
from jax.sharding import PartitionSpec as P

F32 = jnp.float32
BF16 = jnp.bfloat16
VMEM_LIMIT = 16 * 1024 * 1024


def call(body, out, scratch, flops, nbytes):
    return pl.pallas_call(
        body,
        out_shape=out,
        scratch_shapes=scratch,
        compiler_params=pltpu.CompilerParams(vmem_limit_bytes=VMEM_LIMIT),
        cost_estimate=pl.CostEstimate(flops=flops, bytes_accessed=nbytes, transcendentals=0),
    )


def shifted(x, back):
    width = x.shape[-1]
    lane = lax.broadcasted_iota(jnp.int32, x.shape, x.ndim - 1)
    wide = x.astype(F32)
    if back:
        moved = jnp.where(lane == 0, 0.0, pltpu.roll(wide, 1, x.ndim - 1))
    else:
        moved = jnp.where(lane == width - 1, 0.0, pltpu.roll(wide, width - 1, x.ndim - 1))
    return moved.astype(x.dtype)


def fill_padded(pad_ref, before_ref, x, after_ref):
    rows = x.shape[0]
    pad_ref[0] = before_ref[...]
    pad_ref[pl.ds(1, rows)] = x
    pad_ref[rows + 1] = after_ref[...]


def swapped(x):
    return jnp.transpose(x, (1, 0, 2))


def conv_partials(pad_ref, weight_ref, part_ref, flip):
    weight = weight_ref[...]

    def two(step, carry):
        rows = []
        for k in range(2):
            x = pad_ref[2 * step + k]
            rows.append(jnp.concatenate([shifted(x, not flip), x, shifted(x, flip)], axis=0))
        both = jnp.concatenate(rows, axis=1)
        got = jnp.dot(weight, both, preferred_element_type=F32)
        width = got.shape[1] // 2
        part_ref[2 * step] = got[:, :width]
        part_ref[2 * step + 1] = got[:, width:]
        return carry

    lax.fori_loop(0, pad_ref.shape[0] // 2, two, 0, unroll=True)


def forward_body(
    before_ref, x_ref, after_ref, weight_ref, active_ref, slope_ref, pad_ref, part_ref, act_ref
):
    channels, rows, width = x_ref.shape
    fill_padded(pad_ref, before_ref, swapped(x_ref[...]), after_ref)
    conv_partials(pad_ref, weight_ref, part_ref, False)

    def one(row, carry):
        hidden = (
            part_ref[row, :channels]
            + part_ref[row + 1, channels : 2 * channels]
            + part_ref[row + 2, 2 * channels :]
        )
        sigma = 1.0 / (1.0 + jnp.exp(-hidden))
        act_ref[row] = (hidden * sigma).astype(BF16)
        slope_ref[row] = sigma * (1.0 + hidden * (1.0 - sigma))
        return carry

    lax.fori_loop(0, rows, one, 0, unroll=4)
    active_ref[...] = swapped(act_ref[...])


def input_grad_body(before_ref, d_ref, after_ref, weight_ref, cot_ref, out_ref, pad_ref, part_ref, sum_ref):
    rows, channels, width = d_ref.shape
    fill_padded(pad_ref, before_ref, d_ref[...], after_ref)
    conv_partials(pad_ref, weight_ref, part_ref, True)

    def one(row, carry):
        total = (
            part_ref[row + 2, :channels]
            + part_ref[row + 1, channels : 2 * channels]
            + part_ref[row, 2 * channels :]
        )
        sum_ref[row] = total
        return carry

    lax.fori_loop(0, rows, one, 0, unroll=4)
    out_ref[...] = (cot_ref[...].astype(F32) + swapped(sum_ref[...])).astype(BF16)


def chunks_of(tile_shape, body):
    group, rows = tile_shape[1:3]
    per = rows // 16

    def one(index, carry):
        body(index // per, pl.ds(pl.multiple_of((index % per) * 16, 16), 16))
        return carry

    lax.fori_loop(0, group * per, one, 0)


def back_body(coef_ref, cot_ref, back_ref):
    frames, group = cot_ref.shape[:2]

    def one(chan, some):
        cot = [cot_ref[t, chan, some].astype(F32) for t in range(frames)]
        coef = [coef_ref[chan, pl.ds(l, 1)] for l in range(frames)]
        for r in range(frames):
            total = coef[0] * cot[r]
            for t in range(r + 1, frames):
                total = total + coef[t - r] * cot[t]
            back_ref[r, chan, some] = total.astype(BF16)

    chunks_of(cot_ref.shape, one)


def along_body(coef_ref, cot_ref, act_ref, out_ref, sum_ref):
    frames, group, rows, width = cot_ref.shape
    sum_ref[...] = jnp.zeros_like(sum_ref)

    def one(chan, some):
        act = [act_ref[t, chan, some].astype(F32) for t in range(frames)]
        coef = [coef_ref[chan, pl.ds(l, 1)] for l in range(frames)]
        to = pl.ds(pl.multiple_of(chan * rows + some.start, 16), 16)
        for t in range(frames):
            total = coef[0] * act[t]
            for r in range(t):
                total = total + coef[t - r] * act[r]
            out_ref[t, to] = total.astype(BF16)
        cot = [cot_ref[t, chan, some].astype(F32) for t in range(frames)]
        for lag in range(frames):
            total = cot[lag] * act[0]
            for t in range(lag + 1, frames):
                total = total + cot[t] * act[t - lag]
            sum_ref[chan, lag] += total[:8] + total[8:]

    chunks_of(cot_ref.shape, one)
    lane = lax.broadcasted_iota(jnp.int32, (frames, width), 1)
    both = jnp.zeros((frames, width), F32)
    for chan in range(group):
        sums = jnp.sum(jnp.sum(sum_ref[chan], axis=1), axis=1, keepdims=True)
        high = sums.astype(BF16).astype(F32)
        both = jnp.where(lane == chan, high, both)
        both = jnp.where(lane == width // 2 + chan, sums - high, both)
    both = both.astype(BF16)
    for t in range(frames):
        out_ref[t, pl.ds(group * rows, frames)] = both


def block_output_body(x_ref, got_ref, out_ref):
    channels, rows, width = x_ref.shape
    owners = got_ref.shape[0]
    group = channels // owners
    for owner in range(owners):
        for chan in range(group):
            here = owner * group + chan
            along = got_ref[owner, pl.ds(chan * rows, rows)].astype(F32)
            out_ref[here] = (x_ref[here].astype(F32) + along).astype(BF16)


def kernel_sums_body(got_ref, sums_ref):
    owners = got_ref.shape[0]
    lags, channels = sums_ref.shape
    width = got_ref.shape[2]
    group = channels // owners
    lane = lax.broadcasted_iota(jnp.int32, (lags, width), 1)
    total = jnp.zeros((lags, width), F32)
    for owner in range(owners):
        part = got_ref[owner, pl.ds(got_ref.shape[1] - lags, lags)].astype(F32)
        part = part + pltpu.roll(part, width // 2, 1)
        if owner > 0:
            part = pltpu.roll(part, owner * group, 1)
        total = jnp.where(lane // group == owner, part, total)
    sums_ref[...] = total[:, :channels]


def weight_grad_body(
    side_ref, back_ref, slope_ref, pad_ref, dhid_ref, keep_ref, give_ref,
    dpad_ref, grad_ref, pack_ref, turn_ref,
):
    rows, channels, width = slope_ref.shape
    turn_ref[...] = swapped(back_ref[...])
    zero = jnp.zeros((2, channels, width), BF16)
    dpad_ref[pl.ds(0, 2)] = zero
    dpad_ref[pl.ds(rows + 2, 2)] = zero

    def one(row, carry):
        value = (turn_ref[row].astype(F32) * slope_ref[row]).astype(BF16)
        dhid_ref[row] = value
        dpad_ref[row + 2] = value
        return carry

    lax.fori_loop(0, rows, one, 0, unroll=4)
    grad_ref[...] = jnp.zeros_like(grad_ref)

    def two(step, carry):
        left, right = [], []
        for k in range(2):
            row = 2 * step + k
            x = pad_ref[row]
            right.append(jnp.concatenate([shifted(x, True), x, shifted(x, False)], axis=0))
            left.append(jnp.concatenate([dpad_ref[row + 2], dpad_ref[row + 1], dpad_ref[row]], axis=0))
        grad_ref[...] += lax.dot_general(
            jnp.concatenate(left, axis=1),
            jnp.concatenate(right, axis=1),
            (((1,), (1,)), ((), ())),
            preferred_element_type=F32,
        )
        return carry

    lax.fori_loop(0, (rows + 2) // 2, two, 0, unroll=True)
    tall = 3 * channels
    pack_ref[pl.ds(0, tall)] = grad_ref[:, : 2 * channels]
    pack_ref[pl.ds(tall, tall // 2)] = jnp.concatenate(
        [grad_ref[: tall // 2, 2 * channels :], grad_ref[tall // 2 :, 2 * channels :]], axis=1
    )
    half = keep_ref.shape[0]
    done = tall + tall // 2
    if 2 * half > done:
        pack_ref[pl.ds(done, 2 * half - done)] = jnp.zeros((2 * half - done, 2 * channels), F32)
    first = side_ref[pl.ds(0, 1)] > 0
    low, high = pack_ref[pl.ds(0, half)], pack_ref[pl.ds(half, half)]
    keep_ref[...] = jnp.where(first, low, high)
    give_ref[...] = jnp.where(first, high, low)


def unpack_body(gscale, side_ref, mine_ref, other_ref, weight_ref, pack_ref):
    channels = weight_ref.shape[2]
    half = mine_ref.shape[0]
    first = side_ref[pl.ds(0, 1)] > 0
    mine, other = mine_ref[...] * gscale, other_ref[...] * gscale
    pack_ref[pl.ds(0, half)] = jnp.where(first, mine, other)
    pack_ref[pl.ds(half, half)] = jnp.where(first, other, mine)
    tall = 3 * channels
    for a in range(3):
        here = pack_ref[pl.ds(a * channels, channels)]
        weight_ref[a, 0] = here[:, :channels]
        weight_ref[a, 1] = here[:, channels:]
    last = pack_ref[pl.ds(tall, tall // 2)]
    last = jnp.concatenate([last[:, :channels], last[:, channels:]], axis=0)
    for a in range(3):
        weight_ref[a, 2] = last[a * channels : (a + 1) * channels]


def edges(first, last):
    size = lax.axis_size("span")
    if size == 2:
        low = lax.axis_index("span") == 0
        other = swap_cores(jnp.where(low, last, first))
        none = jnp.zeros_like(other)
        return jnp.where(low, none, other), jnp.where(low, other, none)
    up = [(i, (i + 1) % size) for i in range(size - 1)]
    down = [(j, i) for i, j in up]
    return lax.ppermute(last, "span", up), lax.ppermute(first, "span", down)


def tree_sum(parts):
    while len(parts) > 1:
        parts = [parts[i] + parts[i + 1] for i in range(0, len(parts), 2)]
    return parts[0]


def xor_sum(x, axis, steps):
    size = lax.axis_size(axis)
    return tree_sum([x] + [lax.ppermute(x, axis, [(i, i ^ k) for i in range(size)]) for k in steps[1:]])


def swap_cores(x):
    size = lax.axis_size("span")
    return lax.ppermute(x, "span", [(i, i ^ 1) for i in range(size)])


def far_parts(mine, plane):
    size = lax.axis_size("span")
    count = lax.axis_size("tm")
    if size > 2:
        mine = xor_sum(mine, "span", list(range(0, size, 2)))
    steps = range(plane, count, plane)
    return [mine] + [lax.ppermute(mine, "tm", [(i, i ^ k) for i in range(count)]) for k in steps]


def local(frames, cotangent, spatial_weight, temporal_kernel):
    channels, rows, width = frames.shape[1:]
    count = lax.axis_size("tm")
    plane = min(4, count)
    gscale = float(count * rows * lax.axis_size("span") * width) ** (-0.5)
    group = channels // count
    shape = (rows, channels, width)
    tile = (count, group, rows, width)
    area = rows * width
    act_bytes = channels * area * 2
    flops = 18 * channels * channels * area
    half = -(-(9 * channels * channels) // (128 * 16)) * 8
    side = jnp.full((8, 128), 1 - lax.axis_index("span") % 2, F32)
    part = pltpu.VMEM((rows + 2, 3 * channels, width), F32)
    whole = jax.ShapeDtypeStruct(shape, BF16)
    native = jax.ShapeDtypeStruct((channels, rows, width), BF16)
    padded = (rows + 2, channels, width)

    def exchange(x):
        return lax.all_to_all(x, "tm", split_axis=0, concat_axis=0, tiled=True)

    frame, cot = frames[0], cotangent[0]
    cot_tile = exchange(cot.reshape(tile))
    x_before, x_after = edges(frame[:, 0], frame[:, -1])
    weight = spatial_weight.transpose(0, 2, 1, 3).reshape(3 * channels, 3 * channels)
    weight_back = spatial_weight.transpose(0, 3, 1, 2).reshape(3 * channels, 3 * channels)
    coef = lax.dynamic_slice_in_dim(temporal_kernel, lax.axis_index("tm") * group, group, 0)
    coef = jnp.broadcast_to(coef.astype(F32)[:, :, None], (group, count, width))
    active, slope, x = call(
        forward_body,
        (native, jax.ShapeDtypeStruct(shape, F32), jax.ShapeDtypeStruct(padded, BF16)),
        [part, pltpu.VMEM(shape, BF16)],
        flops,
        4 * act_bytes,
    )(x_before, frame, x_after, weight)
    back = call(
        back_body, jax.ShapeDtypeStruct(tile, BF16), [], 17 * channels * area, 2 * act_bytes
    )(coef, cot_tile)
    back, slope = lax.optimization_barrier((back, slope))
    back = exchange(back)
    active, back = lax.optimization_barrier((active, back))
    act_tile = exchange(active.reshape(tile))
    dhidden, keep, give = call(
        weight_grad_body,
        (whole, *[jax.ShapeDtypeStruct((half, 128), F32)] * 2),
        [
            pltpu.VMEM((rows + 4, channels, width), BF16),
            pltpu.VMEM((3 * channels, 3 * channels), F32),
            pltpu.VMEM((2 * half, 128), F32),
            pltpu.VMEM(shape, BF16),
        ],
        flops,
        5 * act_bytes,
    )(side, back.reshape(native.shape), slope, x)
    d_before, d_after = edges(dhidden[0], dhidden[-1])
    input_grad = call(
        input_grad_body,
        native,
        [pltpu.VMEM(padded, BF16), part, pltpu.VMEM(shape, F32)],
        flops,
        4 * act_bytes,
    )(d_before, dhidden, d_after, weight_back, cot)
    weight_mine = keep + swap_cores(give)
    packed = jax.ShapeDtypeStruct((count, group * rows + count, width), BF16)
    along = call(
        along_body,
        packed,
        [pltpu.VMEM((group, count, 8, width), F32)],
        34 * channels * area,
        3 * act_bytes,
    )(coef, cot_tile, act_tile)
    weight_parts = far_parts(weight_mine, plane)
    along, *weight_parts = lax.optimization_barrier((along, *weight_parts))
    along = exchange(along)
    weight_mine = xor_sum(tree_sum(weight_parts), "tm", list(range(plane)))
    weight_mine, input_grad = lax.optimization_barrier((weight_mine, input_grad))
    weight_total = call(
        functools.partial(unpack_body, gscale),
        jax.ShapeDtypeStruct(spatial_weight.shape, F32),
        [pltpu.VMEM((2 * half, 128), F32)],
        0,
        act_bytes,
    )(side, weight_mine, swap_cores(weight_mine))
    kernel_sum = call(
        kernel_sums_body, jax.ShapeDtypeStruct((count, channels), F32), [], 0, 0
    )(along)
    block_output = call(block_output_body, native, [], 0, 0)(frame, along)
    kernel_total = xor_sum(kernel_sum, "span", list(range(lax.axis_size("span")))) * gscale
    return (
        block_output[None],
        input_grad[None],
        weight_total,
        kernel_total.T,
    )


def solution(mesh):
    placed = (P("tm", None, "span", None), P("tm", None, "span", None), P(), P())
    return jax.shard_map(
        local,
        mesh=mesh,
        in_specs=placed,
        out_specs=(P("tm", None, "span", None), P("tm", None, "span", None), P(), P()),
        check_vma=False,
    )
```

```python
import functools

import jax
import jax.numpy as jnp
from jax import lax
from jax.experimental import pallas as pl
from jax.experimental.pallas import tpu as pltpu
from jax.sharding import PartitionSpec as P

F32 = jnp.float32
BF16 = jnp.bfloat16
VMEM_LIMIT = 16 * 1024 * 1024


def call(body, out, scratch, flops, nbytes, hbm_in=(), hbm_out=()):
    def specs(arrays, outside):
        return [
            pl.BlockSpec(memory_space=pltpu.HBM if k in outside else pltpu.VMEM)
            for k in range(len(arrays))
        ]

    def run(*operands):
        return pl.pallas_call(
            body,
            out_shape=out,
            in_specs=specs(operands, hbm_in),
            out_specs=specs(out, hbm_out),
            scratch_shapes=scratch,
            compiler_params=pltpu.CompilerParams(vmem_limit_bytes=VMEM_LIMIT),
            cost_estimate=pl.CostEstimate(flops=flops, bytes_accessed=nbytes, transcendentals=0),
        )(*operands)

    return run


def shifted(x, back):
    width = x.shape[-1]
    lane = lax.broadcasted_iota(jnp.int32, x.shape, x.ndim - 1)
    wide = x.astype(F32)
    if back:
        moved = jnp.where(lane == 0, 0.0, pltpu.roll(wide, 1, x.ndim - 1))
    else:
        moved = jnp.where(lane == width - 1, 0.0, pltpu.roll(wide, width - 1, x.ndim - 1))
    return moved.astype(x.dtype)


def fill_padded(pad_ref, before_ref, x, after_ref):
    rows = x.shape[0]
    pad_ref[0] = before_ref[...]
    pad_ref[pl.ds(1, rows)] = x
    pad_ref[rows + 1] = after_ref[...]


def swapped(x):
    return jnp.transpose(x, (1, 0, 2))


def conv_partials(pad_ref, weight_ref, part_ref, flip):
    weight = weight_ref[...]

    def two(step, carry):
        rows = []
        for k in range(2):
            x = pad_ref[2 * step + k]
            rows.append(jnp.concatenate([shifted(x, not flip), x, shifted(x, flip)], axis=0))
        both = jnp.concatenate(rows, axis=1)
        got = jnp.dot(weight, both, preferred_element_type=F32)
        width = got.shape[1] // 2
        part_ref[2 * step] = got[:, :width]
        part_ref[2 * step + 1] = got[:, width:]
        return carry

    lax.fori_loop(0, pad_ref.shape[0] // 2, two, 0, unroll=True)


def forward_body(
    before_ref, x_ref, after_ref, weight_ref,
    active_ref, slope_ref, pad_ref, part_ref, act_ref,
):
    channels, rows, width = x_ref.shape
    fill_padded(pad_ref, before_ref, swapped(x_ref[...]), after_ref)
    conv_partials(pad_ref, weight_ref, part_ref, False)

    def one(row, carry):
        hidden = (
            part_ref[row, :channels]
            + part_ref[row + 1, channels : 2 * channels]
            + part_ref[row + 2, 2 * channels :]
        )
        sigma = 1.0 / (1.0 + jnp.exp(-hidden))
        act_ref[row] = (hidden * sigma).astype(BF16)
        slope_ref[row] = sigma * (1.0 + hidden * (1.0 - sigma))
        return carry

    lax.fori_loop(0, rows, one, 0, unroll=4)
    active_ref[...] = swapped(act_ref[...])


def input_grad_body(
    before_ref, after_ref, weight_ref, got_ref, slope_ref, cot_ref, out_ref,
    pad_ref, part_ref, sum_ref, turn_ref,
):
    rows, channels, width = slope_ref.shape
    dhidden_rows(got_ref, slope_ref, turn_ref, pad_ref, 1)
    pad_ref[0] = before_ref[...]
    pad_ref[rows + 1] = after_ref[...]
    conv_partials(pad_ref, weight_ref, part_ref, True)

    def one(row, carry):
        total = (
            part_ref[row + 2, :channels]
            + part_ref[row + 1, channels : 2 * channels]
            + part_ref[row, 2 * channels :]
        )
        sum_ref[row] = total
        return carry

    lax.fori_loop(0, rows, one, 0, unroll=4)
    out_ref[...] = (cot_ref[...].astype(F32) + swapped(sum_ref[...])).astype(BF16)


def chunks_of(tile_shape, body):
    group, rows = tile_shape[1:3]
    per = rows // 16

    def one(index, carry):
        body(index // per, pl.ds(pl.multiple_of((index % per) * 16, 16), 16))
        return carry

    lax.fori_loop(0, group * per, one, 0)


def back_body(coef_ref, cot_ref, active_ref, out_ref):
    frames, group = cot_ref.shape[:2]
    for owner in range(frames):
        out_ref[owner, 1] = active_ref[pl.ds(owner * group, group)]

    def one(chan, some):
        cot = [cot_ref[t, chan, some].astype(F32) for t in range(frames)]
        coef = [coef_ref[chan, pl.ds(l, 1)] for l in range(frames)]
        for r in range(frames):
            total = coef[0] * cot[r]
            for t in range(r + 1, frames):
                total = total + coef[t - r] * cot[t]
            out_ref[r, 0, chan, some] = total.astype(BF16)

    chunks_of(cot_ref.shape, one)


def along_body(coef_ref, got_ref, along_ref):
    frames, _, group, rows, width = got_ref.shape

    def one(chan, some):
        act = [got_ref[t, 1, chan, some].astype(F32) for t in range(frames)]
        coef = [coef_ref[chan, pl.ds(l, 1)] for l in range(frames)]
        for t in range(frames):
            total = coef[0] * act[t]
            for r in range(t):
                total = total + coef[t - r] * act[r]
            along_ref[t, chan, some] = total.astype(BF16)

    chunks_of(along_ref.shape, one)


def kernel_sums(cot_ref, got_ref, mine_ref, sum_ref):
    frames, group, rows, width = cot_ref.shape
    sum_ref[...] = jnp.zeros_like(sum_ref)

    def one(chan, some):
        act = [got_ref[t, 1, chan, some].astype(F32) for t in range(frames)]
        cot = [cot_ref[t, chan, some].astype(F32) for t in range(frames)]
        for lag in range(frames):
            total = cot[lag] * act[0]
            for t in range(lag + 1, frames):
                total = total + cot[t] * act[t - lag]
            sum_ref[chan, lag] += total[:8] + total[8:]

    chunks_of(cot_ref.shape, one)
    both = jnp.zeros((frames, width), F32)
    lane = mine_ref[pl.ds(0, 1)]
    for chan in range(group):
        sums = jnp.sum(jnp.sum(sum_ref[chan], axis=1), axis=1, keepdims=True)
        both = jnp.where(lane == chan, sums, both)
    return both


def block_output_body(x_ref, even_ref, odd_ref, out_ref):
    for chan in range(x_ref.shape[0]):
        along = (even_ref, odd_ref)[chan % 2][chan]
        out_ref[chan] = (x_ref[chan].astype(F32) + along.astype(F32)).astype(BF16)


def dhidden_rows(got_ref, slope_ref, turn_ref, to_ref, first):
    rows, channels, width = slope_ref.shape
    turn_ref[...] = swapped(got_ref[:, 0].reshape(channels, rows, width))

    def one(row, carry):
        to_ref[row + first] = (turn_ref[row].astype(F32) * slope_ref[row]).astype(BF16)
        return carry

    lax.fori_loop(0, rows, one, 0, unroll=4)


def weight_grad_body(
    side_ref, mine_ref, got_ref, slope_ref, before_ref, x_ref, after_ref, cot_ref,
    edge_ref, keep_ref, give_ref,
    dpad_ref, grad_ref, pack_ref, turn_ref, pad_ref, sum_ref,
):
    rows, channels, width = slope_ref.shape
    fill_padded(pad_ref, before_ref, swapped(x_ref[...]), after_ref)
    zero = jnp.zeros((2, channels, width), BF16)
    dpad_ref[pl.ds(0, 2)] = zero
    dpad_ref[pl.ds(rows + 2, 2)] = zero
    dhidden_rows(got_ref, slope_ref, turn_ref, dpad_ref, 2)
    edge_ref[0] = dpad_ref[2]
    edge_ref[1] = dpad_ref[rows + 1]
    grad_ref[...] = jnp.zeros_like(grad_ref)

    def two(step, carry):
        left, right = [], []
        for k in range(2):
            row = 2 * step + k
            x = pad_ref[row]
            right.append(jnp.concatenate([shifted(x, True), x, shifted(x, False)], axis=0))
            left.append(jnp.concatenate([dpad_ref[row + 2], dpad_ref[row + 1], dpad_ref[row]], axis=0))
        grad_ref[...] += lax.dot_general(
            jnp.concatenate(left, axis=1),
            jnp.concatenate(right, axis=1),
            (((1,), (1,)), ((), ())),
            preferred_element_type=F32,
        )
        return carry

    lax.fori_loop(0, (rows + 2) // 2, two, 0, unroll=True)
    tall = 3 * channels
    pack_ref[pl.ds(0, tall)] = grad_ref[:, : 2 * channels]
    pack_ref[pl.ds(tall, tall // 2)] = jnp.concatenate(
        [grad_ref[: tall // 2, 2 * channels :], grad_ref[tall // 2 :, 2 * channels :]], axis=1
    )
    half = keep_ref.shape[0]
    done = tall + tall // 2
    sums = kernel_sums(cot_ref, got_ref, mine_ref, sum_ref)
    lags = sums.shape[0] // 2
    pack_ref[pl.ds(done, lags)] = jnp.concatenate(
        [sums[:lags, :channels], sums[lags:, :channels]], axis=1
    )
    done += lags
    if 2 * half > done:
        pack_ref[pl.ds(done, 2 * half - done)] = jnp.zeros((2 * half - done, 2 * channels), F32)
    first = side_ref[pl.ds(0, 1)] > 0
    low, high = pack_ref[pl.ds(0, half)], pack_ref[pl.ds(half, half)]
    keep_ref[...] = jnp.where(first, low, high)
    give_ref[...] = jnp.where(first, high, low)


def unpack_body(gscale, side_ref, mine_ref, other_ref, weight_ref, kernel_ref, pack_ref):
    channels = weight_ref.shape[2]
    half = mine_ref.shape[0]
    first = side_ref[pl.ds(0, 1)] > 0
    mine, other = mine_ref[...] * gscale, other_ref[...] * gscale
    pack_ref[pl.ds(0, half)] = jnp.where(first, mine, other)
    pack_ref[pl.ds(half, half)] = jnp.where(first, other, mine)
    tall = 3 * channels
    for a in range(3):
        here = pack_ref[pl.ds(a * channels, channels)]
        weight_ref[a, 0] = here[:, :channels]
        weight_ref[a, 1] = here[:, channels:]
    last = pack_ref[pl.ds(tall, tall // 2)]
    last = jnp.concatenate([last[:, :channels], last[:, channels:]], axis=0)
    for a in range(3):
        weight_ref[a, 2] = last[a * channels : (a + 1) * channels]
    lags = kernel_ref.shape[0] // 2
    sums = pack_ref[pl.ds(tall + tall // 2, lags)]
    kernel_ref[pl.ds(0, lags)] = sums[:, :channels]
    kernel_ref[pl.ds(lags, lags)] = sums[:, channels:]


def behind(x, other):
    def body(x_ref, other_ref, out_ref):
        pass

    anywhere = pl.BlockSpec(memory_space=pl.ANY)
    return pl.pallas_call(
        body,
        out_shape=jax.ShapeDtypeStruct(x.shape, x.dtype),
        in_specs=[anywhere, anywhere],
        out_specs=anywhere,
        input_output_aliases={0: 0},
    )(x, other)


def edges(first, last):
    size = lax.axis_size("span")
    if size == 2:
        low = lax.axis_index("span") == 0
        other = swap_cores(jnp.where(low, last, first))
        none = jnp.zeros_like(other)
        return jnp.where(low, none, other), jnp.where(low, other, none)
    up = [(i, (i + 1) % size) for i in range(size - 1)]
    down = [(j, i) for i, j in up]
    return lax.ppermute(last, "span", up), lax.ppermute(first, "span", down)


def tree_sum(parts):
    while len(parts) > 1:
        parts = [parts[i] + parts[i + 1] for i in range(0, len(parts), 2)]
    return parts[0]


def xor_sum(x, axis, steps):
    size = lax.axis_size(axis)
    return tree_sum([x] + [lax.ppermute(x, axis, [(i, i ^ k) for i in range(size)]) for k in steps[1:]])


def swap_cores(x):
    size = lax.axis_size("span")
    return lax.ppermute(x, "span", [(i, i ^ 1) for i in range(size)])


def total_over_rest(mine, plane):
    size = lax.axis_size("span")
    count = lax.axis_size("tm")
    if size > 2:
        mine = xor_sum(mine, "span", list(range(0, size, 2)))
    mine = xor_sum(mine, "tm", list(range(0, count, plane)))
    return xor_sum(mine, "tm", list(range(plane)))


def local(frames, cotangent, spatial_weight, temporal_kernel):
    channels, rows, width = frames.shape[1:]
    count = lax.axis_size("tm")
    plane = min(4, count)
    gscale = float(count * rows * lax.axis_size("span") * width) ** (-0.5)
    group = channels // count
    shape = (rows, channels, width)
    tile = (count, group, rows, width)
    area = rows * width
    act_bytes = channels * area * 2
    flops = 18 * channels * channels * area
    half = -(-(9 * channels * channels + count * channels) // (128 * 16)) * 8
    side = jnp.full((8, 128), 1 - lax.axis_index("span") % 2, F32)
    mine = lax.broadcasted_iota(jnp.int32, (8, width), 1) - lax.axis_index("tm") * group
    part = pltpu.VMEM((rows + 2, 3 * channels, width), F32)
    whole = jax.ShapeDtypeStruct(shape, BF16)
    native = jax.ShapeDtypeStruct((channels, rows, width), BF16)
    padded = (rows + 2, channels, width)

    def exchange(x):
        return lax.all_to_all(x, "tm", split_axis=0, concat_axis=0, tiled=True)

    frame, cot = frames[0], cotangent[0]
    cot_tile = exchange(cot.reshape(tile))
    x_before, x_after = edges(frame[:, 0], frame[:, -1])
    weight = spatial_weight.transpose(0, 2, 1, 3).reshape(3 * channels, 3 * channels)
    weight_back = spatial_weight.transpose(0, 3, 1, 2).reshape(3 * channels, 3 * channels)
    coef = lax.dynamic_slice_in_dim(temporal_kernel, lax.axis_index("tm") * group, group, 0)
    weight, weight_back = lax.optimization_barrier((weight, weight_back))
    coef = jnp.broadcast_to(coef.astype(F32)[:, :, None], (group, count, width))
    active, slope = call(
        forward_body,
        (native, jax.ShapeDtypeStruct(shape, F32)),
        [pltpu.VMEM(padded, BF16), part, pltpu.VMEM(shape, BF16)],
        flops,
        4 * act_bytes,
    )(x_before, frame, x_after, weight)
    packed = (count, 2, group, rows, width)
    [out] = call(
        back_body,
        [jax.ShapeDtypeStruct(packed, BF16)],
        [],
        17 * channels * area,
        4 * act_bytes,
    )(coef, cot_tile, active)
    got = exchange(out)
    [along] = call(
        along_body, [jax.ShapeDtypeStruct(tile, BF16)], [], 17 * channels * area, 2 * act_bytes
    )(coef, got)
    d_edges, keep, give = call(
        weight_grad_body,
        (
            jax.ShapeDtypeStruct((2, channels, width), BF16),
            *[jax.ShapeDtypeStruct((half, 128), F32)] * 2,
        ),
        [
            pltpu.VMEM((rows + 4, channels, width), BF16),
            pltpu.VMEM((3 * channels, 3 * channels), F32),
            pltpu.VMEM((2 * half, 128), F32),
            pltpu.VMEM(shape, BF16),
            pltpu.VMEM(padded, BF16),
            pltpu.VMEM((group, count, 8, width), F32),
        ],
        flops,
        5 * act_bytes,
    )(side, mine, got, slope, x_before, frame, x_after, cot_tile)
    d_before, d_after = edges(d_edges[0], d_edges[1])
    [input_grad] = call(
        input_grad_body,
        [native],
        [pltpu.VMEM(padded, BF16), part, pltpu.VMEM(shape, F32), pltpu.VMEM(shape, BF16)],
        flops,
        4 * act_bytes,
    )(d_before, d_after, weight_back, got, slope, cot)
    sums = keep + swap_cores(give)
    along = exchange(behind(along, sums[:8])).reshape(native.shape)
    sums = total_over_rest(sums, plane)
    [block_output] = call(block_output_body, [native], [], channels * area, 3 * act_bytes)(
        frame, along, along
    )
    sums, input_grad = lax.optimization_barrier((sums, input_grad))
    weight_total, kernel_total = call(
        functools.partial(unpack_body, gscale),
        (
            jax.ShapeDtypeStruct(spatial_weight.shape, F32),
            jax.ShapeDtypeStruct((count, channels), F32),
        ),
        [pltpu.VMEM((2 * half, 128), F32)],
        0,
        act_bytes,
    )(side, sums, swap_cores(sums))
    return (
        block_output[None],
        input_grad[None],
        weight_total,
        kernel_total.T,
    )


def solution(mesh):
    placed = (P("tm", None, "span", None), P("tm", None, "span", None), P(), P())
    return jax.shard_map(
        local,
        mesh=mesh,
        in_specs=placed,
        out_specs=(P("tm", None, "span", None), P("tm", None, "span", None), P(), P()),
        check_vma=False,
    )
```

```python
import functools

import jax
import jax.numpy as jnp
from jax import lax
from jax.experimental import pallas as pl
from jax.experimental.pallas import tpu as pltpu
from jax.sharding import PartitionSpec as P

F32 = jnp.float32
BF16 = jnp.bfloat16
VMEM_LIMIT = 16 * 1024 * 1024


def call(body, out, scratch, flops, nbytes, hbm_in=(), hbm_out=()):
    def specs(arrays, outside):
        return [
            pl.BlockSpec(memory_space=pltpu.HBM if k in outside else pltpu.VMEM)
            for k in range(len(arrays))
        ]

    def run(*operands):
        return pl.pallas_call(
            body,
            out_shape=out,
            in_specs=specs(operands, hbm_in),
            out_specs=specs(out, hbm_out),
            scratch_shapes=scratch,
            compiler_params=pltpu.CompilerParams(vmem_limit_bytes=VMEM_LIMIT),
            cost_estimate=pl.CostEstimate(flops=flops, bytes_accessed=nbytes, transcendentals=0),
        )(*operands)

    return run


def shifted(x, back):
    width = x.shape[-1]
    lane = lax.broadcasted_iota(jnp.int32, x.shape, x.ndim - 1)
    wide = x.astype(F32)
    if back:
        moved = jnp.where(lane == 0, 0.0, pltpu.roll(wide, 1, x.ndim - 1))
    else:
        moved = jnp.where(lane == width - 1, 0.0, pltpu.roll(wide, width - 1, x.ndim - 1))
    return moved.astype(x.dtype)


def fill_padded(pad_ref, before_ref, x, after_ref):
    rows = x.shape[0]
    pad_ref[0] = before_ref[...]
    pad_ref[pl.ds(1, rows)] = x
    pad_ref[rows + 1] = after_ref[...]


def swapped(x):
    return jnp.transpose(x, (1, 0, 2))


def conv_partials(pad_ref, weight_ref, part_ref, flip):
    weight = weight_ref[...]

    def two(step, carry):
        rows = []
        for k in range(2):
            x = pad_ref[2 * step + k]
            rows.append(jnp.concatenate([shifted(x, not flip), x, shifted(x, flip)], axis=0))
        both = jnp.concatenate(rows, axis=1)
        got = jnp.dot(weight, both, preferred_element_type=F32)
        width = got.shape[1] // 2
        part_ref[2 * step] = got[:, :width]
        part_ref[2 * step + 1] = got[:, width:]
        return carry

    lax.fori_loop(0, pad_ref.shape[0] // 2, two, 0, unroll=True)


def forward_body(
    before_ref, x_ref, after_ref, weight_ref,
    active_ref, slope_ref, pad_ref, part_ref, act_ref,
):
    channels, rows, width = x_ref.shape
    fill_padded(pad_ref, before_ref, swapped(x_ref[...]), after_ref)
    conv_partials(pad_ref, weight_ref, part_ref, False)

    def one(row, carry):
        hidden = (
            part_ref[row, :channels]
            + part_ref[row + 1, channels : 2 * channels]
            + part_ref[row + 2, 2 * channels :]
        )
        sigma = 1.0 / (1.0 + jnp.exp(-hidden))
        act_ref[row] = (hidden * sigma).astype(BF16)
        slope_ref[row] = sigma * (1.0 + hidden * (1.0 - sigma))
        return carry

    lax.fori_loop(0, rows, one, 0, unroll=4)
    active_ref[...] = swapped(act_ref[...])


def input_grad_body(
    before_ref, after_ref, weight_ref, got_ref, slope_ref, cot_ref, out_ref,
    pad_ref, part_ref, sum_ref, turn_ref,
):
    rows, channels, width = slope_ref.shape
    dhidden_rows(got_ref, slope_ref, turn_ref, pad_ref, 1)
    pad_ref[0] = before_ref[...]
    pad_ref[rows + 1] = after_ref[...]
    conv_partials(pad_ref, weight_ref, part_ref, True)

    def one(row, carry):
        total = (
            part_ref[row + 2, :channels]
            + part_ref[row + 1, channels : 2 * channels]
            + part_ref[row, 2 * channels :]
        )
        sum_ref[row] = total
        return carry

    lax.fori_loop(0, rows, one, 0, unroll=4)
    out_ref[...] = (cot_ref[...].astype(F32) + swapped(sum_ref[...])).astype(BF16)


def chunks_of(tile_shape, body):
    group, rows = tile_shape[1:3]
    per = rows // 16

    def one(index, carry):
        body(index // per, pl.ds(pl.multiple_of((index % per) * 16, 16), 16))
        return carry

    lax.fori_loop(0, group * per, one, 0)


def back_body(coef_ref, cot_ref, active_ref, out_ref):
    frames, group = cot_ref.shape[:2]
    for owner in range(frames):
        out_ref[owner, 1] = active_ref[pl.ds(owner * group, group)]

    def one(chan, some):
        cot = [cot_ref[t, chan, some].astype(F32) for t in range(frames)]
        coef = [coef_ref[chan, pl.ds(l, 1)] for l in range(frames)]
        for r in range(frames):
            total = coef[0] * cot[r]
            for t in range(r + 1, frames):
                total = total + coef[t - r] * cot[t]
            out_ref[r, 0, chan, some] = total.astype(BF16)

    chunks_of(cot_ref.shape, one)


def along_body(coef_ref, got_ref, along_ref):
    frames, _, group, rows, width = got_ref.shape

    def one(chan, some):
        act = [got_ref[t, 1, chan, some].astype(F32) for t in range(frames)]
        coef = [coef_ref[chan, pl.ds(l, 1)] for l in range(frames)]
        for t in range(frames):
            total = coef[0] * act[t]
            for r in range(t):
                total = total + coef[t - r] * act[r]
            along_ref[t, chan, some] = total.astype(BF16)

    chunks_of(along_ref.shape, one)


def kernel_sums(cot_ref, got_ref, mine_ref, sum_ref):
    frames, group, rows, width = cot_ref.shape
    sum_ref[...] = jnp.zeros_like(sum_ref)

    def one(chan, some):
        act = [got_ref[t, 1, chan, some].astype(F32) for t in range(frames)]
        cot = [cot_ref[t, chan, some].astype(F32) for t in range(frames)]
        for lag in range(frames):
            total = cot[lag] * act[0]
            for t in range(lag + 1, frames):
                total = total + cot[t] * act[t - lag]
            sum_ref[chan, lag] += total[:8] + total[8:]

    chunks_of(cot_ref.shape, one)
    both = jnp.zeros((frames, width), F32)
    lane = mine_ref[pl.ds(0, 1)]
    for chan in range(group):
        sums = jnp.sum(jnp.sum(sum_ref[chan], axis=1), axis=1, keepdims=True)
        both = jnp.where(lane == chan, sums, both)
    return both


def block_output_body(x_ref, even_ref, odd_ref, out_ref):
    for chan in range(x_ref.shape[0]):
        along = (even_ref, odd_ref)[chan % 2][chan]
        out_ref[chan] = (x_ref[chan].astype(F32) + along.astype(F32)).astype(BF16)


def dhidden_rows(got_ref, slope_ref, turn_ref, to_ref, first):
    rows, channels, width = slope_ref.shape
    turn_ref[...] = swapped(got_ref[:, 0].reshape(channels, rows, width))

    def one(row, carry):
        to_ref[row + first] = (turn_ref[row].astype(F32) * slope_ref[row]).astype(BF16)
        return carry

    lax.fori_loop(0, rows, one, 0, unroll=4)


def weight_grad_body(
    side_ref, mine_ref, got_ref, slope_ref, before_ref, x_ref, after_ref, cot_ref,
    edge_ref, keep_ref, give_ref,
    dpad_ref, grad_ref, pack_ref, turn_ref, pad_ref, sum_ref,
):
    rows, channels, width = slope_ref.shape
    fill_padded(pad_ref, before_ref, swapped(x_ref[...]), after_ref)
    zero = jnp.zeros((2, channels, width), BF16)
    dpad_ref[pl.ds(0, 2)] = zero
    dpad_ref[pl.ds(rows + 2, 2)] = zero
    dhidden_rows(got_ref, slope_ref, turn_ref, dpad_ref, 2)
    edge_ref[0] = dpad_ref[2]
    edge_ref[1] = dpad_ref[rows + 1]
    left, right = [], []
    for row in range(rows + 2):
        x = pad_ref[row]
        right.append(jnp.concatenate([shifted(x, True), x, shifted(x, False)], axis=0))
        left.append(jnp.concatenate([dpad_ref[row + 2], dpad_ref[row + 1], dpad_ref[row]], axis=0))
    grad_ref[...] = lax.dot_general(
        jnp.concatenate(left, axis=1),
        jnp.concatenate(right, axis=1),
        (((1,), (1,)), ((), ())),
        preferred_element_type=F32,
    )
    tall = 3 * channels
    pack_ref[pl.ds(0, tall)] = grad_ref[:, : 2 * channels]
    pack_ref[pl.ds(tall, tall // 2)] = jnp.concatenate(
        [grad_ref[: tall // 2, 2 * channels :], grad_ref[tall // 2 :, 2 * channels :]], axis=1
    )
    half = keep_ref.shape[0]
    done = tall + tall // 2
    sums = kernel_sums(cot_ref, got_ref, mine_ref, sum_ref)
    lags = sums.shape[0] // 2
    pack_ref[pl.ds(done, lags)] = jnp.concatenate(
        [sums[:lags, :channels], sums[lags:, :channels]], axis=1
    )
    done += lags
    if 2 * half > done:
        pack_ref[pl.ds(done, 2 * half - done)] = jnp.zeros((2 * half - done, 2 * channels), F32)
    first = side_ref[pl.ds(0, 1)] > 0
    low, high = pack_ref[pl.ds(0, half)], pack_ref[pl.ds(half, half)]
    keep_ref[...] = jnp.where(first, low, high)
    give_ref[...] = jnp.where(first, high, low)


def unpack_body(gscale, side_ref, mine_ref, other_ref, weight_ref, kernel_ref, pack_ref):
    channels = weight_ref.shape[2]
    half = mine_ref.shape[0]
    first = side_ref[pl.ds(0, 1)] > 0
    mine, other = mine_ref[...] * gscale, other_ref[...] * gscale
    pack_ref[pl.ds(0, half)] = jnp.where(first, mine, other)
    pack_ref[pl.ds(half, half)] = jnp.where(first, other, mine)
    tall = 3 * channels
    for a in range(3):
        here = pack_ref[pl.ds(a * channels, channels)]
        weight_ref[a, 0] = here[:, :channels]
        weight_ref[a, 1] = here[:, channels:]
    last = pack_ref[pl.ds(tall, tall // 2)]
    last = jnp.concatenate([last[:, :channels], last[:, channels:]], axis=0)
    for a in range(3):
        weight_ref[a, 2] = last[a * channels : (a + 1) * channels]
    lags = kernel_ref.shape[0] // 2
    sums = pack_ref[pl.ds(tall + tall // 2, lags)]
    kernel_ref[pl.ds(0, lags)] = sums[:, :channels]
    kernel_ref[pl.ds(lags, lags)] = sums[:, channels:]


def edges(first, last):
    size = lax.axis_size("span")
    if size == 2:
        low = lax.axis_index("span") == 0
        other = swap_cores(jnp.where(low, last, first))
        none = jnp.zeros_like(other)
        return jnp.where(low, none, other), jnp.where(low, other, none)
    up = [(i, (i + 1) % size) for i in range(size - 1)]
    down = [(j, i) for i, j in up]
    return lax.ppermute(last, "span", up), lax.ppermute(first, "span", down)


def tree_sum(parts):
    while len(parts) > 1:
        parts = [parts[i] + parts[i + 1] for i in range(0, len(parts), 2)]
    return parts[0]


def xor_sum(x, axis, steps):
    size = lax.axis_size(axis)
    return tree_sum([x] + [lax.ppermute(x, axis, [(i, i ^ k) for i in range(size)]) for k in steps[1:]])


def swap_cores(x):
    size = lax.axis_size("span")
    return lax.ppermute(x, "span", [(i, i ^ 1) for i in range(size)])


def over_planes(mine, plane):
    size = lax.axis_size("span")
    count = lax.axis_size("tm")
    if size > 2:
        mine = xor_sum(mine, "span", list(range(0, size, 2)))
    steps = range(plane, count, plane)
    return [mine] + [lax.ppermute(mine, "tm", [(i, i ^ k) for i in range(count)]) for k in steps]


def local(frames, cotangent, spatial_weight, temporal_kernel):
    channels, rows, width = frames.shape[1:]
    count = lax.axis_size("tm")
    plane = min(4, count)
    gscale = float(count * rows * lax.axis_size("span") * width) ** (-0.5)
    group = channels // count
    shape = (rows, channels, width)
    tile = (count, group, rows, width)
    area = rows * width
    act_bytes = channels * area * 2
    flops = 18 * channels * channels * area
    half = -(-(9 * channels * channels + count * channels) // (128 * 16)) * 8
    side = jnp.full((8, 128), 1 - lax.axis_index("span") % 2, F32)
    mine = lax.broadcasted_iota(jnp.int32, (8, width), 1) - lax.axis_index("tm") * group
    part = pltpu.VMEM((rows + 2, 3 * channels, width), F32)
    whole = jax.ShapeDtypeStruct(shape, BF16)
    native = jax.ShapeDtypeStruct((channels, rows, width), BF16)
    padded = (rows + 2, channels, width)

    def exchange(x):
        return lax.all_to_all(x, "tm", split_axis=0, concat_axis=0, tiled=True)

    frame, cot = frames[0], cotangent[0]
    cot_tile = exchange(cot.reshape(tile))
    x_before, x_after = edges(frame[:, 0], frame[:, -1])
    weight = spatial_weight.transpose(0, 2, 1, 3).reshape(3 * channels, 3 * channels)
    weight_back = spatial_weight.transpose(0, 3, 1, 2).reshape(3 * channels, 3 * channels)
    coef = lax.dynamic_slice_in_dim(temporal_kernel, lax.axis_index("tm") * group, group, 0)
    weight, weight_back = lax.optimization_barrier((weight, weight_back))
    coef = jnp.broadcast_to(coef.astype(F32)[:, :, None], (group, count, width))
    active, slope = call(
        forward_body,
        (native, jax.ShapeDtypeStruct(shape, F32)),
        [pltpu.VMEM(padded, BF16), part, pltpu.VMEM(shape, BF16)],
        flops,
        4 * act_bytes,
    )(x_before, frame, x_after, weight)
    packed = (count, 2, group, rows, width)
    [out] = call(
        back_body,
        [jax.ShapeDtypeStruct(packed, BF16)],
        [],
        17 * channels * area,
        4 * act_bytes,
    )(coef, cot_tile, active)
    got = exchange(out)
    [along] = call(
        along_body, [jax.ShapeDtypeStruct(tile, BF16)], [], 17 * channels * area, 2 * act_bytes
    )(coef, got)
    d_edges, keep, give = call(
        weight_grad_body,
        (
            jax.ShapeDtypeStruct((2, channels, width), BF16),
            *[jax.ShapeDtypeStruct((half, 128), F32)] * 2,
        ),
        [
            pltpu.VMEM((rows + 4, channels, width), BF16),
            pltpu.VMEM((3 * channels, 3 * channels), F32),
            pltpu.VMEM((2 * half, 128), F32),
            pltpu.VMEM(shape, BF16),
            pltpu.VMEM(padded, BF16),
            pltpu.VMEM((group, count, 8, width), F32),
        ],
        flops,
        5 * act_bytes,
    )(side, mine, got, slope, x_before, frame, x_after, cot_tile)
    d_before, d_after = edges(d_edges[0], d_edges[1])
    [input_grad] = call(
        input_grad_body,
        [native],
        [pltpu.VMEM(padded, BF16), part, pltpu.VMEM(shape, F32), pltpu.VMEM(shape, BF16)],
        flops,
        4 * act_bytes,
    )(d_before, d_after, weight_back, got, slope, cot)
    received = swap_cores(give)
    planes = over_planes(keep + received, plane)
    along, received = lax.optimization_barrier((along, received))
    along = exchange(along).reshape(native.shape)
    sums = xor_sum(tree_sum(planes), "tm", list(range(plane)))
    [block_output] = call(block_output_body, [native], [], channels * area, 3 * act_bytes)(
        frame, along, along
    )
    sums, input_grad = lax.optimization_barrier((sums, input_grad))
    weight_total, kernel_total = call(
        functools.partial(unpack_body, gscale),
        (
            jax.ShapeDtypeStruct(spatial_weight.shape, F32),
            jax.ShapeDtypeStruct((count, channels), F32),
        ),
        [pltpu.VMEM((2 * half, 128), F32)],
        0,
        act_bytes,
    )(side, sums, swap_cores(sums))
    return (
        block_output[None],
        input_grad[None],
        weight_total,
        kernel_total.T,
    )


def solution(mesh):
    placed = (P("tm", None, "span", None), P("tm", None, "span", None), P(), P())
    return jax.shard_map(
        local,
        mesh=mesh,
        in_specs=placed,
        out_specs=(P("tm", None, "span", None), P("tm", None, "span", None), P(), P()),
        check_vma=False,
    )
```

```python
import functools

import jax
import jax.numpy as jnp
from jax import lax
from jax.experimental import pallas as pl
from jax.experimental.pallas import tpu as pltpu
from jax.sharding import PartitionSpec as P

F32 = jnp.float32
BF16 = jnp.bfloat16
VMEM_LIMIT = 16 * 1024 * 1024


def call(body, out, scratch, flops, nbytes, hbm_in=(), hbm_out=(), alias=None):
    def specs(arrays, outside):
        return [
            pl.BlockSpec(memory_space=pl.ANY if k in outside else pltpu.VMEM)
            for k in range(len(arrays))
        ]

    def run(*operands):
        return pl.pallas_call(
            body,
            out_shape=out,
            in_specs=specs(operands, hbm_in),
            out_specs=specs(out, hbm_out),
            scratch_shapes=scratch,
            input_output_aliases=alias or {},
            compiler_params=pltpu.CompilerParams(vmem_limit_bytes=VMEM_LIMIT),
            cost_estimate=pl.CostEstimate(flops=flops, bytes_accessed=nbytes, transcendentals=0),
        )(*operands)

    return run


def in_place(body, coef, values, base):
    vmem, anywhere = pl.BlockSpec(memory_space=pltpu.VMEM), pl.BlockSpec(memory_space=pl.ANY)
    frames, (group, rows, width) = base.shape[0], base.shape[-3:]
    return pl.pallas_call(
        body,
        out_shape=jax.ShapeDtypeStruct(base.shape, BF16),
        in_specs=[vmem, vmem, anywhere],
        out_specs=anywhere,
        scratch_shapes=[
            pltpu.VMEM((group, frames, rows, width), BF16),
            pltpu.SemaphoreType.DMA((group,)),
        ],
        input_output_aliases={2: 0},
        compiler_params=pltpu.CompilerParams(vmem_limit_bytes=VMEM_LIMIT),
        cost_estimate=pl.CostEstimate(
            flops=17 * group * rows * width * frames,
            bytes_accessed=4 * group * rows * width * frames,
            transcendentals=0,
        ),
    )(coef, values, base)


def shifted(x, back):
    width = x.shape[-1]
    lane = lax.broadcasted_iota(jnp.int32, x.shape, x.ndim - 1)
    wide = x.astype(F32)
    if back:
        moved = jnp.where(lane == 0, 0.0, pltpu.roll(wide, 1, x.ndim - 1))
    else:
        moved = jnp.where(lane == width - 1, 0.0, pltpu.roll(wide, width - 1, x.ndim - 1))
    return moved.astype(x.dtype)


def fill_padded(pad_ref, before_ref, x, after_ref):
    rows = x.shape[0]
    pad_ref[0] = before_ref[...]
    pad_ref[pl.ds(1, rows)] = x
    pad_ref[rows + 1] = after_ref[...]


def swapped(x):
    return jnp.transpose(x, (1, 0, 2))


def conv_partials(pad_ref, weight_ref, part_ref, flip):
    weight = weight_ref[...]

    def two(step, carry):
        rows = []
        for k in range(2):
            x = pad_ref[2 * step + k]
            rows.append(jnp.concatenate([shifted(x, not flip), x, shifted(x, flip)], axis=0))
        both = jnp.concatenate(rows, axis=1)
        got = jnp.dot(weight, both, preferred_element_type=F32)
        width = got.shape[1] // 2
        part_ref[2 * step] = got[:, :width]
        part_ref[2 * step + 1] = got[:, width:]
        return carry

    lax.fori_loop(0, pad_ref.shape[0] // 2, two, 0, unroll=True)


def forward_body(
    before_ref, x_ref, after_ref, weight_ref, blank_ref,
    base_ref, slope_ref, pad_ref, part_ref, act_ref, turn_ref, sem,
):
    channels, rows, width = x_ref.shape
    fill_padded(pad_ref, before_ref, swapped(x_ref[...]), after_ref)
    conv_partials(pad_ref, weight_ref, part_ref, False)

    def one(row, carry):
        hidden = (
            part_ref[row, :channels]
            + part_ref[row + 1, channels : 2 * channels]
            + part_ref[row + 2, 2 * channels :]
        )
        sigma = 1.0 / (1.0 + jnp.exp(-hidden))
        act_ref[row] = (hidden * sigma).astype(BF16)
        slope_ref[row] = sigma * (1.0 + hidden * (1.0 - sigma))
        return carry

    lax.fori_loop(0, rows, one, 0, unroll=4)
    turn_ref[...] = swapped(act_ref[...]).reshape(turn_ref.shape)
    send = pltpu.make_async_copy(turn_ref, base_ref.at[:, 1], sem)
    send.start()
    send.wait()


def input_grad_body(
    before_ref, after_ref, weight_ref, got_ref, slope_ref, cot_ref, out_ref,
    pad_ref, part_ref, sum_ref, turn_ref,
):
    rows, channels, width = slope_ref.shape
    dhidden_rows(got_ref, slope_ref, turn_ref, pad_ref, 1)
    pad_ref[0] = before_ref[...]
    pad_ref[rows + 1] = after_ref[...]
    conv_partials(pad_ref, weight_ref, part_ref, True)

    def one(row, carry):
        total = (
            part_ref[row + 2, :channels]
            + part_ref[row + 1, channels : 2 * channels]
            + part_ref[row, 2 * channels :]
        )
        sum_ref[row] = total
        return carry

    lax.fori_loop(0, rows, one, 0, unroll=4)
    out_ref[...] = (cot_ref[...].astype(F32) + swapped(sum_ref[...])).astype(BF16)


def chunks_of(tile_shape, body):
    group, rows = tile_shape[1:3]
    per = rows // 16

    def one(index, carry):
        body(index // per, pl.ds(pl.multiple_of((index % per) * 16, 16), 16))
        return carry

    lax.fori_loop(0, group * per, one, 0)


def toeplitz_chunk(coef_ref, chan, values, store, forward):
    frames = len(values)
    coef = [coef_ref[chan, pl.ds(l, 1)] for l in range(frames)]
    for t in range(frames):
        total = coef[0] * values[t]
        for r in range(t) if forward else range(t + 1, frames):
            total = total + coef[abs(t - r)] * values[r]
        store(t, total.astype(BF16))


def sums_to_hbm(coef_ref, load, targets, held_ref, sems, forward):
    group, frames, rows, width = held_ref.shape
    sends = []
    for chan in range(group):
        for start in range(0, rows, 16):
            some = pl.ds(start, 16)
            values = [load(t, chan, some).astype(F32) for t in range(frames)]

            def store(t, value, chan=chan, some=some):
                held_ref[chan, t, some] = value

            toeplitz_chunk(coef_ref, chan, values, store, forward)
        sends.append(pltpu.make_async_copy(held_ref.at[chan], targets[chan], sems.at[chan]))
        sends[-1].start()
    for send in sends:
        send.wait()


def back_body(coef_ref, cot_ref, base_ref, out_ref, held_ref, sems):
    targets = [out_ref.at[:, 0, chan] for chan in range(held_ref.shape[0])]
    sums_to_hbm(coef_ref, lambda t, c, s: cot_ref[t, c, s], targets, held_ref, sems, False)


def along_body(coef_ref, got_ref, along_ref):
    frames, _, group, rows, width = got_ref.shape

    def one(chan, some):
        act = [got_ref[t, 1, chan, some].astype(F32) for t in range(frames)]
        coef = [coef_ref[chan, pl.ds(l, 1)] for l in range(frames)]
        for t in range(frames):
            total = coef[0] * act[t]
            for r in range(t):
                total = total + coef[t - r] * act[r]
            along_ref[t, chan, some] = total.astype(BF16)

    chunks_of(along_ref.shape, one)


def kernel_sums(cot_ref, got_ref, mine_ref, sum_ref):
    frames, group, rows, width = cot_ref.shape
    sum_ref[...] = jnp.zeros_like(sum_ref)

    def one(chan, some):
        act = [got_ref[t, 1, chan, some].astype(F32) for t in range(frames)]
        cot = [cot_ref[t, chan, some].astype(F32) for t in range(frames)]
        for lag in range(frames):
            total = cot[lag] * act[0]
            for t in range(lag + 1, frames):
                total = total + cot[t] * act[t - lag]
            sum_ref[chan, lag] += total[:8] + total[8:]

    chunks_of(cot_ref.shape, one)
    both = jnp.zeros((frames, width), F32)
    lane = mine_ref[pl.ds(0, 1)]
    for chan in range(group):
        sums = jnp.sum(jnp.sum(sum_ref[chan], axis=1), axis=1, keepdims=True)
        both = jnp.where(lane == chan, sums, both)
    return both


def block_output_body(x_ref, even_ref, odd_ref, out_ref):
    for chan in range(x_ref.shape[0]):
        along = (even_ref, odd_ref)[chan % 2][chan]
        out_ref[chan] = (x_ref[chan].astype(F32) + along.astype(F32)).astype(BF16)


def dhidden_rows(got_ref, slope_ref, turn_ref, to_ref, first):
    rows, channels, width = slope_ref.shape
    turn_ref[...] = swapped(got_ref[:, 0].reshape(channels, rows, width))

    def one(row, carry):
        to_ref[row + first] = (turn_ref[row].astype(F32) * slope_ref[row]).astype(BF16)
        return carry

    lax.fori_loop(0, rows, one, 0, unroll=4)


def weight_grad_body(
    side_ref, mine_ref, got_ref, slope_ref, before_ref, x_ref, after_ref, cot_ref,
    edge_ref, keep_ref, give_ref,
    dpad_ref, grad_ref, pack_ref, turn_ref, pad_ref, sum_ref,
):
    rows, channels, width = slope_ref.shape
    fill_padded(pad_ref, before_ref, swapped(x_ref[...]), after_ref)
    zero = jnp.zeros((2, channels, width), BF16)
    dpad_ref[pl.ds(0, 2)] = zero
    dpad_ref[pl.ds(rows + 2, 2)] = zero
    dhidden_rows(got_ref, slope_ref, turn_ref, dpad_ref, 2)
    edge_ref[0] = dpad_ref[2]
    edge_ref[1] = dpad_ref[rows + 1]
    left, right = [], []
    for row in range(rows + 2):
        x = pad_ref[row]
        right.append(jnp.concatenate([shifted(x, True), x, shifted(x, False)], axis=0))
        left.append(jnp.concatenate([dpad_ref[row + 2], dpad_ref[row + 1], dpad_ref[row]], axis=0))
    grad_ref[...] = lax.dot_general(
        jnp.concatenate(left, axis=1),
        jnp.concatenate(right, axis=1),
        (((1,), (1,)), ((), ())),
        preferred_element_type=F32,
    )
    tall = 3 * channels
    pack_ref[pl.ds(0, tall)] = grad_ref[:, : 2 * channels]
    pack_ref[pl.ds(tall, tall // 2)] = jnp.concatenate(
        [grad_ref[: tall // 2, 2 * channels :], grad_ref[tall // 2 :, 2 * channels :]], axis=1
    )
    half = keep_ref.shape[0]
    done = tall + tall // 2
    sums = kernel_sums(cot_ref, got_ref, mine_ref, sum_ref)
    lags = sums.shape[0] // 2
    pack_ref[pl.ds(done, lags)] = jnp.concatenate(
        [sums[:lags, :channels], sums[lags:, :channels]], axis=1
    )
    done += lags
    if 2 * half > done:
        pack_ref[pl.ds(done, 2 * half - done)] = jnp.zeros((2 * half - done, 2 * channels), F32)
    first = side_ref[pl.ds(0, 1)] > 0
    low, high = pack_ref[pl.ds(0, half)], pack_ref[pl.ds(half, half)]
    keep_ref[...] = jnp.where(first, low, high)
    give_ref[...] = jnp.where(first, high, low)


def unpack_body(gscale, side_ref, mine_ref, other_ref, weight_ref, kernel_ref, pack_ref):
    channels = weight_ref.shape[2]
    half = mine_ref.shape[0]
    first = side_ref[pl.ds(0, 1)] > 0
    mine, other = mine_ref[...] * gscale, other_ref[...] * gscale
    pack_ref[pl.ds(0, half)] = jnp.where(first, mine, other)
    pack_ref[pl.ds(half, half)] = jnp.where(first, other, mine)
    tall = 3 * channels
    for a in range(3):
        here = pack_ref[pl.ds(a * channels, channels)]
        weight_ref[a, 0] = here[:, :channels]
        weight_ref[a, 1] = here[:, channels:]
    last = pack_ref[pl.ds(tall, tall // 2)]
    last = jnp.concatenate([last[:, :channels], last[:, channels:]], axis=0)
    for a in range(3):
        weight_ref[a, 2] = last[a * channels : (a + 1) * channels]
    lags = kernel_ref.shape[0] // 2
    sums = pack_ref[pl.ds(tall + tall // 2, lags)]
    kernel_ref[pl.ds(0, lags)] = sums[:, :channels]
    kernel_ref[pl.ds(lags, lags)] = sums[:, channels:]


def edges(first, last):
    size = lax.axis_size("span")
    if size == 2:
        low = lax.axis_index("span") == 0
        other = swap_cores(jnp.where(low, last, first))
        none = jnp.zeros_like(other)
        return jnp.where(low, none, other), jnp.where(low, other, none)
    up = [(i, (i + 1) % size) for i in range(size - 1)]
    down = [(j, i) for i, j in up]
    return lax.ppermute(last, "span", up), lax.ppermute(first, "span", down)


def tree_sum(parts):
    while len(parts) > 1:
        parts = [parts[i] + parts[i + 1] for i in range(0, len(parts), 2)]
    return parts[0]


def xor_sum(x, axis, steps):
    size = lax.axis_size(axis)
    return tree_sum([x] + [lax.ppermute(x, axis, [(i, i ^ k) for i in range(size)]) for k in steps[1:]])


def swap_cores(x):
    size = lax.axis_size("span")
    return lax.ppermute(x, "span", [(i, i ^ 1) for i in range(size)])


def over_planes(mine, plane):
    size = lax.axis_size("span")
    count = lax.axis_size("tm")
    if size > 2:
        mine = xor_sum(mine, "span", list(range(0, size, 2)))
    steps = range(plane, count, plane)
    return [mine] + [lax.ppermute(mine, "tm", [(i, i ^ k) for i in range(count)]) for k in steps]


def local(frames, cotangent, spatial_weight, temporal_kernel):
    channels, rows, width = frames.shape[1:]
    count = lax.axis_size("tm")
    plane = min(4, count)
    gscale = float(count * rows * lax.axis_size("span") * width) ** (-0.5)
    group = channels // count
    shape = (rows, channels, width)
    tile = (count, group, rows, width)
    area = rows * width
    act_bytes = channels * area * 2
    flops = 18 * channels * channels * area
    half = -(-(9 * channels * channels + count * channels) // (128 * 16)) * 8
    side = jnp.full((8, 128), 1 - lax.axis_index("span") % 2, F32)
    mine = lax.broadcasted_iota(jnp.int32, (8, width), 1) - lax.axis_index("tm") * group
    part = pltpu.VMEM((rows + 2, 3 * channels, width), F32)
    whole = jax.ShapeDtypeStruct(shape, BF16)
    native = jax.ShapeDtypeStruct((channels, rows, width), BF16)
    padded = (rows + 2, channels, width)

    def exchange(x):
        return lax.all_to_all(x, "tm", split_axis=0, concat_axis=0, tiled=True)

    frame, cot = frames[0], cotangent[0]
    cot_tile = exchange(cot.reshape(tile))
    x_before, x_after = edges(frame[:, 0], frame[:, -1])
    weight = spatial_weight.transpose(0, 2, 1, 3).reshape(3 * channels, 3 * channels)
    weight_back = spatial_weight.transpose(0, 3, 1, 2).reshape(3 * channels, 3 * channels)
    coef = lax.dynamic_slice_in_dim(temporal_kernel, lax.axis_index("tm") * group, group, 0)
    weight, weight_back = lax.optimization_barrier((weight, weight_back))
    coef = jnp.broadcast_to(coef.astype(F32)[:, :, None], (group, count, width))
    packed = (count, 2, group, rows, width)
    base, slope = call(
        forward_body,
        (jax.ShapeDtypeStruct(packed, BF16), jax.ShapeDtypeStruct(shape, F32)),
        [
            pltpu.VMEM(padded, BF16),
            part,
            pltpu.VMEM(shape, BF16),
            pltpu.VMEM(tile, BF16),
            pltpu.SemaphoreType.DMA,
        ],
        flops,
        4 * act_bytes,
        hbm_in=(4,),
        hbm_out=(0,),
        alias={4: 0},
    )(x_before, frame, x_after, weight, jnp.zeros(packed, BF16))
    out = in_place(back_body, coef, cot_tile, base)
    got = exchange(out)
    [along] = call(
        along_body, [jax.ShapeDtypeStruct(tile, BF16)], [], 17 * channels * area, 2 * act_bytes
    )(coef, got)
    d_edges, keep, give = call(
        weight_grad_body,
        (
            jax.ShapeDtypeStruct((2, channels, width), BF16),
            *[jax.ShapeDtypeStruct((half, 128), F32)] * 2,
        ),
        [
            pltpu.VMEM((rows + 4, channels, width), BF16),
            pltpu.VMEM((3 * channels, 3 * channels), F32),
            pltpu.VMEM((2 * half, 128), F32),
            pltpu.VMEM(shape, BF16),
            pltpu.VMEM(padded, BF16),
            pltpu.VMEM((group, count, 8, width), F32),
        ],
        flops,
        5 * act_bytes,
    )(side, mine, got, slope, x_before, frame, x_after, cot_tile)
    d_before, d_after = edges(d_edges[0], d_edges[1])
    [input_grad] = call(
        input_grad_body,
        [native],
        [pltpu.VMEM(padded, BF16), part, pltpu.VMEM(shape, F32), pltpu.VMEM(shape, BF16)],
        flops,
        4 * act_bytes,
    )(d_before, d_after, weight_back, got, slope, cot)
    received = swap_cores(give)
    planes = over_planes(keep + received, plane)
    along, received = lax.optimization_barrier((along, received))
    along = exchange(along).reshape(native.shape)
    sums = xor_sum(tree_sum(planes), "tm", list(range(plane)))
    [block_output] = call(block_output_body, [native], [], channels * area, 3 * act_bytes)(
        frame, along, along
    )
    sums, input_grad = lax.optimization_barrier((sums, input_grad))
    weight_total, kernel_total = call(
        functools.partial(unpack_body, gscale),
        (
            jax.ShapeDtypeStruct(spatial_weight.shape, F32),
            jax.ShapeDtypeStruct((count, channels), F32),
        ),
        [pltpu.VMEM((2 * half, 128), F32)],
        0,
        act_bytes,
    )(side, sums, swap_cores(sums))
    return (
        block_output[None],
        input_grad[None],
        weight_total,
        kernel_total.T,
    )


def solution(mesh):
    placed = (P("tm", None, "span", None), P("tm", None, "span", None), P(), P())
    return jax.shard_map(
        local,
        mesh=mesh,
        in_specs=placed,
        out_specs=(P("tm", None, "span", None), P("tm", None, "span", None), P(), P()),
        check_vma=False,
    )
```

```python
import functools

import jax
import jax.numpy as jnp
from jax import lax
from jax.experimental import pallas as pl
from jax.experimental.pallas import tpu as pltpu
from jax.sharding import PartitionSpec as P

F32 = jnp.float32
BF16 = jnp.bfloat16
VMEM_LIMIT = 16 * 1024 * 1024


def call(body, out, scratch, flops, nbytes, hbm_in=(), hbm_out=(), alias=None):
    def specs(arrays, outside):
        return [
            pl.BlockSpec(memory_space=pl.ANY if k in outside else pltpu.VMEM)
            for k in range(len(arrays))
        ]

    def run(*operands):
        return pl.pallas_call(
            body,
            out_shape=out,
            in_specs=specs(operands, hbm_in),
            out_specs=specs(out, hbm_out),
            scratch_shapes=scratch,
            input_output_aliases=alias or {},
            compiler_params=pltpu.CompilerParams(vmem_limit_bytes=VMEM_LIMIT),
            cost_estimate=pl.CostEstimate(flops=flops, bytes_accessed=nbytes, transcendentals=0),
        )(*operands)

    return run


def in_place(body, coef, values, base):
    vmem, anywhere = pl.BlockSpec(memory_space=pltpu.VMEM), pl.BlockSpec(memory_space=pl.ANY)
    frames, (group, rows, width) = base.shape[0], base.shape[-3:]
    return pl.pallas_call(
        body,
        out_shape=jax.ShapeDtypeStruct(base.shape, BF16),
        in_specs=[vmem, vmem, anywhere],
        out_specs=anywhere,
        scratch_shapes=[
            pltpu.VMEM((group, frames, rows, width), BF16),
            pltpu.SemaphoreType.DMA((group,)),
        ],
        input_output_aliases={2: 0},
        compiler_params=pltpu.CompilerParams(vmem_limit_bytes=VMEM_LIMIT),
        cost_estimate=pl.CostEstimate(
            flops=17 * group * rows * width * frames,
            bytes_accessed=4 * group * rows * width * frames,
            transcendentals=0,
        ),
    )(coef, values, base)


def shifted(x, back):
    width = x.shape[-1]
    lane = lax.broadcasted_iota(jnp.int32, x.shape, x.ndim - 1)
    wide = x.astype(F32)
    if back:
        moved = jnp.where(lane == 0, 0.0, pltpu.roll(wide, 1, x.ndim - 1))
    else:
        moved = jnp.where(lane == width - 1, 0.0, pltpu.roll(wide, width - 1, x.ndim - 1))
    return moved.astype(x.dtype)


def fill_padded(pad_ref, before_ref, x, after_ref):
    rows = x.shape[0]
    pad_ref[0] = before_ref[...]
    pad_ref[pl.ds(1, rows)] = x
    pad_ref[rows + 1] = after_ref[...]


def swapped(x):
    return jnp.transpose(x, (1, 0, 2))


def conv_partials(pad_ref, weight_ref, part_ref, flip):
    weight = weight_ref[...]

    def two(step, carry):
        rows = []
        for k in range(2):
            x = pad_ref[2 * step + k]
            rows.append(jnp.concatenate([shifted(x, not flip), x, shifted(x, flip)], axis=0))
        both = jnp.concatenate(rows, axis=1)
        got = jnp.dot(weight, both, preferred_element_type=F32)
        width = got.shape[1] // 2
        part_ref[2 * step] = got[:, :width]
        part_ref[2 * step + 1] = got[:, width:]
        return carry

    lax.fori_loop(0, pad_ref.shape[0] // 2, two, 0, unroll=True)


def forward_body(
    before_ref, x_ref, after_ref, weight_ref, blank_ref,
    base_ref, slope_ref, pad_ref, part_ref, act_ref, turn_ref, sem,
):
    channels, rows, width = x_ref.shape
    fill_padded(pad_ref, before_ref, swapped(x_ref[...]), after_ref)
    conv_partials(pad_ref, weight_ref, part_ref, False)

    def one(row, carry):
        hidden = (
            part_ref[row, :channels]
            + part_ref[row + 1, channels : 2 * channels]
            + part_ref[row + 2, 2 * channels :]
        )
        sigma = 1.0 / (1.0 + jnp.exp(-hidden))
        act_ref[row] = (hidden * sigma).astype(BF16)
        slope_ref[row] = sigma * (1.0 + hidden * (1.0 - sigma))
        return carry

    lax.fori_loop(0, rows, one, 0, unroll=4)
    turn_ref[...] = swapped(act_ref[...]).reshape(turn_ref.shape)
    send = pltpu.make_async_copy(turn_ref, base_ref.at[:, 1], sem)
    send.start()
    send.wait()


def input_grad_body(
    before_ref, after_ref, weight_ref, got_ref, slope_ref, cot_ref, out_ref,
    pad_ref, part_ref, sum_ref, turn_ref,
):
    rows, channels, width = slope_ref.shape
    dhidden_rows(got_ref, slope_ref, turn_ref, pad_ref, 1)
    pad_ref[0] = before_ref[...]
    pad_ref[rows + 1] = after_ref[...]
    conv_partials(pad_ref, weight_ref, part_ref, True)

    def one(row, carry):
        total = (
            part_ref[row + 2, :channels]
            + part_ref[row + 1, channels : 2 * channels]
            + part_ref[row, 2 * channels :]
        )
        sum_ref[row] = total
        return carry

    lax.fori_loop(0, rows, one, 0, unroll=4)
    out_ref[...] = (cot_ref[...].astype(F32) + swapped(sum_ref[...])).astype(BF16)


def chunks_of(tile_shape, body):
    group, rows = tile_shape[1:3]
    per = rows // 16

    def one(index, carry):
        body(index // per, pl.ds(pl.multiple_of((index % per) * 16, 16), 16))
        return carry

    lax.fori_loop(0, group * per, one, 0)


def toeplitz_chunk(coef_ref, chan, values, store, forward):
    frames = len(values)
    coef = [coef_ref[chan, pl.ds(l, 1)] for l in range(frames)]
    for t in range(frames):
        total = coef[0] * values[t]
        for r in range(t) if forward else range(t + 1, frames):
            total = total + coef[abs(t - r)] * values[r]
        store(t, total.astype(BF16))


def sums_to_hbm(coef_ref, load, targets, held_ref, sems, forward):
    group, frames, rows, width = held_ref.shape
    sends = []
    for chan in range(group):
        for start in range(0, rows, 16):
            some = pl.ds(start, 16)
            values = [load(t, chan, some).astype(F32) for t in range(frames)]

            def store(t, value, chan=chan, some=some):
                held_ref[chan, t, some] = value

            toeplitz_chunk(coef_ref, chan, values, store, forward)
        sends.append(pltpu.make_async_copy(held_ref.at[chan], targets[chan], sems.at[chan]))
        sends[-1].start()
    for send in sends:
        send.wait()


def back_body(coef_ref, cot_ref, base_ref, out_ref, held_ref, sems):
    targets = [out_ref.at[:, 0, chan] for chan in range(held_ref.shape[0])]
    sums_to_hbm(coef_ref, lambda t, c, s: cot_ref[t, c, s], targets, held_ref, sems, False)


def along_body(coef_ref, mine_ref, keep_ref, cot_ref, got_ref, along_ref, pack_ref, sum_ref):
    frames, group, rows, width = cot_ref.shape
    channels = width // 2
    sum_ref[...] = jnp.zeros_like(sum_ref)

    def one(chan, some):
        act = [got_ref[t, 1, chan, some].astype(F32) for t in range(frames)]
        coef = [coef_ref[chan, pl.ds(l, 1)] for l in range(frames)]
        for t in range(frames):
            total = coef[0] * act[t]
            for r in range(t):
                total = total + coef[t - r] * act[r]
            along_ref[t, chan, some] = total.astype(BF16)
        cot = [cot_ref[t, chan, some].astype(F32) for t in range(frames)]
        for lag in range(frames):
            total = cot[lag] * act[0]
            for t in range(lag + 1, frames):
                total = total + cot[t] * act[t - lag]
            sum_ref[chan, lag] += total[:8] + total[8:]

    chunks_of(cot_ref.shape, one)
    both = jnp.zeros((frames, width), F32)
    lane = mine_ref[pl.ds(0, 1)]
    for chan in range(group):
        sums = jnp.sum(jnp.sum(sum_ref[chan], axis=1), axis=1, keepdims=True)
        both = jnp.where(lane == chan, sums, both)
    lags = frames // 2
    half = keep_ref.shape[0]
    pack_ref[pl.ds(0, half)] = keep_ref[...]
    pack_ref[pl.ds(half, lags)] = jnp.concatenate([both[:lags, :channels], both[lags:, :channels]], axis=1)


def block_output_body(x_ref, even_ref, odd_ref, out_ref):
    for chan in range(x_ref.shape[0]):
        along = (even_ref, odd_ref)[chan % 2][chan]
        out_ref[chan] = (x_ref[chan].astype(F32) + along.astype(F32)).astype(BF16)


def dhidden_rows(got_ref, slope_ref, turn_ref, to_ref, first):
    rows, channels, width = slope_ref.shape
    turn_ref[...] = swapped(got_ref[:, 0].reshape(channels, rows, width))

    def one(row, carry):
        to_ref[row + first] = (turn_ref[row].astype(F32) * slope_ref[row]).astype(BF16)
        return carry

    lax.fori_loop(0, rows, one, 0, unroll=4)


def weight_grad_body(
    side_ref, got_ref, slope_ref, before_ref, x_ref, after_ref,
    edge_ref, keep_ref, give_ref,
    dpad_ref, grad_ref, pack_ref, turn_ref, pad_ref,
):
    rows, channels, width = slope_ref.shape
    fill_padded(pad_ref, before_ref, swapped(x_ref[...]), after_ref)
    zero = jnp.zeros((2, channels, width), BF16)
    dpad_ref[pl.ds(0, 2)] = zero
    dpad_ref[pl.ds(rows + 2, 2)] = zero
    dhidden_rows(got_ref, slope_ref, turn_ref, dpad_ref, 2)
    edge_ref[0] = dpad_ref[2]
    edge_ref[1] = dpad_ref[rows + 1]
    left, right = [], []
    for row in range(rows + 2):
        x = pad_ref[row]
        right.append(jnp.concatenate([shifted(x, True), x, shifted(x, False)], axis=0))
        left.append(jnp.concatenate([dpad_ref[row + 2], dpad_ref[row + 1], dpad_ref[row]], axis=0))
    grad_ref[...] = lax.dot_general(
        jnp.concatenate(left, axis=1),
        jnp.concatenate(right, axis=1),
        (((1,), (1,)), ((), ())),
        preferred_element_type=F32,
    )
    tall = 3 * channels
    pack_ref[pl.ds(0, tall)] = grad_ref[:, : 2 * channels]
    pack_ref[pl.ds(tall, tall // 2)] = jnp.concatenate(
        [grad_ref[: tall // 2, 2 * channels :], grad_ref[tall // 2 :, 2 * channels :]], axis=1
    )
    half = keep_ref.shape[0]
    done = tall + tall // 2
    if 2 * half > done:
        pack_ref[pl.ds(done, 2 * half - done)] = jnp.zeros((2 * half - done, 2 * channels), F32)
    first = side_ref[pl.ds(0, 1)] > 0
    low, high = pack_ref[pl.ds(0, half)], pack_ref[pl.ds(half, half)]
    keep_ref[...] = jnp.where(first, low, high)
    give_ref[pl.ds(0, half)] = jnp.where(first, high, low)
    rest = give_ref.shape[0] - half
    give_ref[pl.ds(half, rest)] = jnp.zeros((rest, 2 * channels), F32)


def unpack_body(gscale, side_ref, mine_ref, other_ref, weight_ref, kernel_ref, pack_ref):
    channels = weight_ref.shape[2]
    half = pack_ref.shape[0] // 2
    first = side_ref[pl.ds(0, 1)] > 0
    mine, other = mine_ref[pl.ds(0, half)] * gscale, other_ref[pl.ds(0, half)] * gscale
    pack_ref[pl.ds(0, half)] = jnp.where(first, mine, other)
    pack_ref[pl.ds(half, half)] = jnp.where(first, other, mine)
    tall = 3 * channels
    for a in range(3):
        here = pack_ref[pl.ds(a * channels, channels)]
        weight_ref[a, 0] = here[:, :channels]
        weight_ref[a, 1] = here[:, channels:]
    last = pack_ref[pl.ds(tall, tall // 2)]
    last = jnp.concatenate([last[:, :channels], last[:, channels:]], axis=0)
    for a in range(3):
        weight_ref[a, 2] = last[a * channels : (a + 1) * channels]
    lags = kernel_ref.shape[0] // 2
    sums = (mine_ref[pl.ds(half, lags)] + other_ref[pl.ds(half, lags)]) * gscale
    kernel_ref[pl.ds(0, lags)] = sums[:, :channels]
    kernel_ref[pl.ds(lags, lags)] = sums[:, channels:]


def edges(first, last):
    size = lax.axis_size("span")
    if size == 2:
        low = lax.axis_index("span") == 0
        other = swap_cores(jnp.where(low, last, first))
        none = jnp.zeros_like(other)
        return jnp.where(low, none, other), jnp.where(low, other, none)
    up = [(i, (i + 1) % size) for i in range(size - 1)]
    down = [(j, i) for i, j in up]
    return lax.ppermute(last, "span", up), lax.ppermute(first, "span", down)


def tree_sum(parts):
    while len(parts) > 1:
        parts = [parts[i] + parts[i + 1] for i in range(0, len(parts), 2)]
    return parts[0]


def xor_sum(x, axis, steps):
    size = lax.axis_size(axis)
    return tree_sum([x] + [lax.ppermute(x, axis, [(i, i ^ k) for i in range(size)]) for k in steps[1:]])


def swap_cores(x):
    size = lax.axis_size("span")
    return lax.ppermute(x, "span", [(i, i ^ 1) for i in range(size)])


def over_planes(mine, plane):
    size = lax.axis_size("span")
    count = lax.axis_size("tm")
    if size > 2:
        mine = xor_sum(mine, "span", list(range(0, size, 2)))
    steps = range(plane, count, plane)
    return [mine] + [lax.ppermute(mine, "tm", [(i, i ^ k) for i in range(count)]) for k in steps]


def local(frames, cotangent, spatial_weight, temporal_kernel):
    channels, rows, width = frames.shape[1:]
    count = lax.axis_size("tm")
    plane = min(4, count)
    gscale = float(count * rows * lax.axis_size("span") * width) ** (-0.5)
    group = channels // count
    shape = (rows, channels, width)
    tile = (count, group, rows, width)
    area = rows * width
    act_bytes = channels * area * 2
    flops = 18 * channels * channels * area
    half = -(-(9 * channels * channels) // (128 * 16)) * 8
    side = jnp.full((8, 128), 1 - lax.axis_index("span") % 2, F32)
    mine = lax.broadcasted_iota(jnp.int32, (8, width), 1) - lax.axis_index("tm") * group
    part = pltpu.VMEM((rows + 2, 3 * channels, width), F32)
    whole = jax.ShapeDtypeStruct(shape, BF16)
    native = jax.ShapeDtypeStruct((channels, rows, width), BF16)
    padded = (rows + 2, channels, width)

    def exchange(x):
        return lax.all_to_all(x, "tm", split_axis=0, concat_axis=0, tiled=True)

    frame, cot = frames[0], cotangent[0]
    cot_tile = exchange(cot.reshape(tile))
    x_before, x_after = edges(frame[:, 0], frame[:, -1])
    weight = spatial_weight.transpose(0, 2, 1, 3).reshape(3 * channels, 3 * channels)
    weight_back = spatial_weight.transpose(0, 3, 1, 2).reshape(3 * channels, 3 * channels)
    coef = lax.dynamic_slice_in_dim(temporal_kernel, lax.axis_index("tm") * group, group, 0)
    weight, weight_back = lax.optimization_barrier((weight, weight_back))
    coef = jnp.broadcast_to(coef.astype(F32)[:, :, None], (group, count, width))
    packed = (count, 2, group, rows, width)
    base, slope = call(
        forward_body,
        (jax.ShapeDtypeStruct(packed, BF16), jax.ShapeDtypeStruct(shape, F32)),
        [
            pltpu.VMEM(padded, BF16),
            part,
            pltpu.VMEM(shape, BF16),
            pltpu.VMEM(tile, BF16),
            pltpu.SemaphoreType.DMA,
        ],
        flops,
        4 * act_bytes,
        hbm_in=(4,),
        hbm_out=(0,),
        alias={4: 0},
    )(x_before, frame, x_after, weight, jnp.zeros(packed, BF16))
    out = in_place(back_body, coef, cot_tile, base)
    got = exchange(out)
    d_edges, keep, give = call(
        weight_grad_body,
        (
            jax.ShapeDtypeStruct((2, channels, width), BF16),
            jax.ShapeDtypeStruct((half, 128), F32),
            jax.ShapeDtypeStruct((half + count // 2, 128), F32),
        ),
        [
            pltpu.VMEM((rows + 4, channels, width), BF16),
            pltpu.VMEM((3 * channels, 3 * channels), F32),
            pltpu.VMEM((2 * half, 128), F32),
            pltpu.VMEM(shape, BF16),
            pltpu.VMEM(padded, BF16),
        ],
        flops,
        5 * act_bytes,
    )(side, got, slope, x_before, frame, x_after)
    along, kept = call(
        along_body,
        (jax.ShapeDtypeStruct(tile, BF16), jax.ShapeDtypeStruct((half + count // 2, width), F32)),
        [pltpu.VMEM((group, count, 8, width), F32)],
        34 * channels * area,
        3 * act_bytes,
    )(coef, mine, keep, cot_tile, got)
    d_before, d_after = edges(d_edges[0], d_edges[1])
    [input_grad] = call(
        input_grad_body,
        [native],
        [pltpu.VMEM(padded, BF16), part, pltpu.VMEM(shape, F32), pltpu.VMEM(shape, BF16)],
        flops,
        4 * act_bytes,
    )(d_before, d_after, weight_back, got, slope, cot)
    received = swap_cores(give)
    planes = over_planes(kept + received, plane)
    along, received = lax.optimization_barrier((along, received))
    along = exchange(along).reshape(native.shape)
    sums = xor_sum(tree_sum(planes), "tm", list(range(plane)))
    [block_output] = call(block_output_body, [native], [], channels * area, 3 * act_bytes)(
        frame, along, along
    )
    sums, input_grad = lax.optimization_barrier((sums, input_grad))
    weight_total, kernel_total = call(
        functools.partial(unpack_body, gscale),
        (
            jax.ShapeDtypeStruct(spatial_weight.shape, F32),
            jax.ShapeDtypeStruct((count, channels), F32),
        ),
        [pltpu.VMEM((2 * half, 128), F32)],
        0,
        act_bytes,
    )(side, sums, swap_cores(sums))
    return (
        block_output[None],
        input_grad[None],
        weight_total,
        kernel_total.T,
    )


def solution(mesh):
    placed = (P("tm", None, "span", None), P("tm", None, "span", None), P(), P())
    return jax.shard_map(
        local,
        mesh=mesh,
        in_specs=placed,
        out_specs=(P("tm", None, "span", None), P("tm", None, "span", None), P(), P()),
        check_vma=False,
    )
```
